256 devices in a mesh: row: 32 (over x, y, core), col: 8 (over z).
Axes of the slice: x: 4, y: 4, z: 8, core: 2. Of those that a mesh axis runs over, the one named last changes fastest.
Arguments:
- in_map: bfloat16 [512, 256, 256], P('row', 'col'), may hold values from -6 to 6
- tile_w: bfloat16 [3, 3, 256, 256], replicated, may hold values from -0.125 to 0.125
- head_w1: bfloat16 [3, 3, 256, 256], replicated, may hold values from -0.125 to 0.125
- head_w2: bfloat16 [3, 3, 256, 256], replicated, may hold values from -0.125 to 0.125
- box_row: int32 [512, 8], P('row', 'col'), may hold values from 0 to 2
- box_col: int32 [512, 8], P('row', 'col'), may hold values from 0 to 18
- box_target: int32 [512, 8], P('row', 'col'), may hold values from -1 to 31, as said below
- head_cot: bfloat16 [128, 8, 14, 14, 256], P('row', 'col'), may hold values from -6 to 6
Outputs:
- grad_map: bfloat16 [512, 256, 256], P('row', 'col')
- grad_w1: float32 [3, 3, 256, 256], replicated
- grad_w2: float32 [3, 3, 256, 256], replicated
The draws below stay inside these ranges and needn't reach their ends.
Inputs may be any that keep to these rules, and one draw needn't show every extreme that they name: `box_target`: within each row r of tiles, every head slot d * 4 + h (d below 8, h below 4) is named by exactly one tile slot, and empty slots hold -1. A tile names at most 2 head slots of one device, so it holds at most 16 boxes; in every row of tiles one tile holds 16 boxes, 2 for each device of the row.
All inputs are finite; a program needn't handle non-finite values.
Results may differ from the reference program's by a relative error of at most 0.012.
Values may be sent and summed in bfloat16 or wider, within the bound.
A program may use at most 64 MiB of HBM per device.

```python
import math
import jax
import jax.numpy as jnp
from jax import lax

C = 256
BOX = 14
TR = 16
TC = 32
HB = 4
CAP = 2
SLOTS = 16
H = 512
W = 256
N_ROW = 32
N_COL = 8


def draw_box_target(key, part):

    def one_row(row_key):
        keys = jax.random.split(row_key, 5)
        heavy = jax.random.randint(keys[0], (), 0, N_COL).astype(jnp.int32)
        others = jax.random.randint(keys[1], (N_COL, HB - CAP), 0, N_COL - 1).astype(jnp.int32)
        others = others + (others >= heavy).astype(jnp.int32)
        source = jnp.concatenate([jnp.full((N_COL, CAP), heavy, jnp.int32), others], axis=1)
        order = jax.vmap(lambda k: jax.random.permutation(k, HB))(jax.random.split(keys[2], N_COL)).astype(jnp.int32)
        target = jnp.arange(N_COL, dtype=jnp.int32)[:, None] * HB + order
        source = source.reshape(-1)
        target = target.reshape(-1)
        priority = jax.random.permutation(keys[3], N_COL * HB).astype(jnp.int32)
        same_source = source[:, None] == source[None, :]
        ranking = jnp.sum(same_source & (priority[None, :] < priority[:, None]), axis=1).astype(jnp.int32)
        slot_perm = jax.vmap(lambda k: jax.random.permutation(k, SLOTS))(jax.random.split(keys[4], N_COL)).astype(jnp.int32)
        slot_of = slot_perm[source, ranking]
        table = jnp.full((N_COL, SLOTS), -1, jnp.int32).at[source, slot_of].set(target)
        return table.T
    tables = jax.vmap(one_row)(jax.random.split(jax.random.fold_in(key, 7), N_ROW))
    return tables.reshape(N_ROW * SLOTS, N_COL)


def with_ends(values, key, smallest, high):
    spot = [jax.random.randint(jax.random.fold_in(key, axis), (), 0, length) for axis, length in enumerate(values.shape)]
    main_axis = values.shape.index(max(values.shape))
    beside = spot[:main_axis] + [(spot[main_axis] + 1) % values.shape[main_axis]] + spot[main_axis + 1:]
    return values.at[tuple(spot)].set(smallest).at[tuple(beside)].set(high)


def block_scale(rng, dims, shards, least, top_value):
    gain, own = 1.0, jax.random.fold_in(rng, 6)
    for axis_at, blocks in shards:
        heights = jnp.exp(jax.random.uniform(jax.random.fold_in(own, axis_at), (blocks,), jnp.float32, least / len(shards), top_value / len(shards)))
        gain = gain * jnp.repeat(heights, dims[axis_at] // blocks).reshape([-1 if axis == axis_at else 1 for axis in range(len(dims))])
    return gain


def centred(own_key, shape, width, limit, shards=(), kind=jnp.bfloat16):
    result = jax.random.normal(own_key, shape, jnp.float32) * width
    if len(shards) > 0:
        result = block_scale(own_key, shape, shards, -0.22, 0.18) * result
    return jnp.clip(result, min=-limit, max=limit).astype(kind)


def setup_inputs(seed: int = 0) -> dict:
    splits = jax.random.split(jax.random.key(seed), 9)
    return {
        "in_map": centred(splits[0], (H, W, C), 1.0, 6.0, ((0, 32), (1, 8))),
        "tile_w": centred(splits[1], (3, 3, C, C), (9 * C) ** -0.5, 0.125),
        "head_w1": centred(splits[2], (3, 3, C, C), (9 * C) ** -0.5, 0.125),
        "head_w2": centred(splits[3], (3, 3, C, C), (9 * C) ** -0.5, 0.125),
        "box_row": with_ends(jax.random.randint(splits[4], (N_ROW * SLOTS, N_COL), 0, TR - BOX + 1), jax.random.fold_in(splits[4], 1), 0, TR - BOX).astype(jnp.int32),
        "box_col": with_ends(jax.random.randint(splits[5], (N_ROW * SLOTS, N_COL), 0, TC - BOX + 1), jax.random.fold_in(splits[5], 1), 0, TC - BOX).astype(jnp.int32),
        "box_target": draw_box_target(jax.random.fold_in(splits[8], 71), 0),
        "head_cot": centred(splits[7], (N_ROW * HB, N_COL, BOX, BOX, C), 1.0, 6.0, ((0, 32), (1, 8))),
    }


HIGHEST = lax.Precision.HIGHEST
LAYOUT = ('NHWC', 'HWIO', 'NHWC')

def conv_same(inputs, kernel):
    return lax.conv_general_dilated(inputs.astype(jnp.float32), kernel.astype(jnp.float32), (1, 1), ((1, 1), (1, 1)), dimension_numbers=LAYOUT, precision=HIGHEST)

def flip_weights(kernel):
    return jnp.transpose(jnp.flip(kernel, (0, 1)), (0, 1, 3, 2))

def silu_slope(values):
    sigma = jax.nn.sigmoid(values)
    return sigma * (1.0 + values * (1.0 - sigma))

def weight_grad(inputs, deltas):
    channels = inputs.shape[-1]
    box_side = inputs.shape[1]
    padded = jnp.pad(inputs.astype(jnp.float32), ((0, 0), (1, 1), (1, 1), (0, 0)))
    flat_delta = deltas.astype(jnp.float32).reshape(-1, channels)
    blocks = []
    for shift_y in range(3):
        for shift_x in range(3):
            window = padded[:, shift_y:shift_y + box_side, shift_x:shift_x + box_side, :].reshape(-1, channels)
            blocks.append(jnp.dot(window.T, flat_delta, precision=HIGHEST))
    return jnp.stack(blocks).reshape(3, 3, channels, channels)

def reference(in_map, tile_w, head_w1, head_w2, box_row, box_col, box_target, head_cot):
    preact = conv_same(in_map[None], tile_w)[0]
    feature = jax.nn.silu(preact).astype(jnp.bfloat16)
    flat_target = box_target.reshape(N_ROW, SLOTS * N_COL)
    wanted = jnp.arange(N_COL * HB, dtype=jnp.int32)
    positions = jnp.arange(SLOTS * N_COL, dtype=jnp.int32)
    matches = flat_target[:, None, :] == wanted[None, :, None]
    source = lax.optimization_barrier(jnp.sum(jnp.where(matches, positions[None, None, :], 0), axis=2)).astype(jnp.int32)
    local_y = jnp.take_along_axis(box_row.reshape(N_ROW, SLOTS * N_COL), source, axis=1)
    local_x = jnp.take_along_axis(box_col.reshape(N_ROW, SLOTS * N_COL), source, axis=1)
    anchor_y = (jnp.arange(N_ROW, dtype=jnp.int32)[:, None] * TR + local_y).reshape(-1).astype(jnp.int32)
    anchor_x = (source % N_COL * TC + local_x).reshape(-1).astype(jnp.int32)
    zero_index = jnp.zeros((), jnp.int32)
    crops = jax.vmap(lambda y, x: lax.dynamic_slice(feature, (y, x, zero_index), (BOX, BOX, C)))(anchor_y, anchor_x)
    cotangent = head_cot.reshape(N_ROW, HB, N_COL, BOX, BOX, C).transpose(0, 2, 1, 3, 4, 5).reshape(-1, BOX, BOX, C)
    pre_one = conv_same(crops, head_w1)
    hidden = jax.nn.silu(pre_one).astype(jnp.bfloat16)
    pre_two = conv_same(hidden, head_w2)
    delta_two = (cotangent.astype(jnp.float32) * silu_slope(pre_two)).astype(jnp.bfloat16)
    delta_one = (conv_same(delta_two, flip_weights(head_w2)) * silu_slope(pre_one)).astype(jnp.bfloat16)
    box_grads = conv_same(delta_one, flip_weights(head_w1)).astype(jnp.bfloat16)
    factor = 1.0 / math.sqrt(N_ROW * N_COL * HB * BOX * BOX)
    grad_w1 = weight_grad(crops, delta_one) * factor
    grad_w2 = weight_grad(hidden, delta_two) * factor
    offsets = jnp.arange(BOX, dtype=jnp.int32)
    row_index = anchor_y[:, None, None] + offsets[None, :, None]
    col_index = anchor_x[:, None, None] + offsets[None, None, :]
    box_total = jnp.zeros((N_ROW * TR, N_COL * TC, C), jnp.float32).at[row_index, col_index].add(box_grads.astype(jnp.float32))
    delta_map = (box_total * silu_slope(preact)).astype(jnp.bfloat16)
    grad_map = conv_same(delta_map[None], flip_weights(tile_w))[0].astype(jnp.bfloat16)
    return (grad_map, grad_w1, grad_w2)
```

```python
import math

import jax
import jax.numpy as jnp
from jax import lax
from jax.experimental import pallas as pl
from jax.experimental.pallas import tpu as pltpu
from jax.sharding import PartitionSpec as P

MESH = pl.DeviceIdType.MESH
BF = jnp.bfloat16
F32 = jnp.float32
NZ = 8
NX = 4
NY = 4
NROW = 32
PX = 512
HALF = 256
POS = 256
CH = 256
K_HALO = 0
K_TAB = 16
K_AG = 23
K_RS = 37
K_AR = 51
AR_N = 28
N_SEM = K_AR + 2 * AR_N


def silu_slope(values):
    sigma = jax.nn.sigmoid(values)
    return sigma * (1.0 + values * (1.0 - sigma))


def mm(a, b):
    return jnp.dot(a, b, preferred_element_type=F32)


def kernel(
    in_ref, tw_ref, w1_ref, w2_ref, brow_ref, bcol_ref, btgt_ref, cot_ref,
    gmap_ref, gsum_ref,
    xf, xp, x3m, slope_map, scol, hrow, hcol, hl, hr,
    tab, gcol, grow, feats, acc, xc3, xh3, d23, d13, slope1, cotp, xt,
    twt, w1t, w2t, bg, rs_s, rs_r, dm,
    own, snd, rc, s1, r1, t2, s2, r2, t3, s3, r3, zb,
    ssem, rsem,
):
    row = lax.axis_index("row")
    me = lax.axis_index("col")
    px = row // 8
    py = lax.rem(row // 2, NY)
    core = lax.rem(row, 2)

    def at_x(d):
        return (lax.rem(px + d, NX) * 8 + py * 2 + core, me)

    def at_y(d):
        return (px * 8 + lax.rem(py + d, NY) * 2 + core, me)

    def at_z(d):
        return (row, lax.rem(me + d + NZ, NZ))

    sibling = (row + 1 - 2 * core, me)

    def near(dr, dc):
        return (lax.rem(row + dr + NROW, NROW), lax.rem(me + dc + NZ, NZ))

    live = {}

    def send(src, dst, k, dev):
        copy = pltpu.make_async_remote_copy(
            src_ref=src, dst_ref=dst, send_sem=ssem.at[k], recv_sem=rsem.at[k],
            device_id=dev, device_id_type=MESH,
        )
        copy.start()
        live[k] = copy

    def got(k):
        live[k].wait_recv()

    halo_dirs = [(1, 0), (-1, 0), (1, 1), (0, 1), (-1, 1), (1, -1), (0, -1), (-1, -1)]

    barrier = pltpu.get_barrier_semaphore()
    partners = [near(*d) for d in halo_dirs]
    partners += [at_z(d) for d in range(2, 7)]
    partners += [at_x(d) for d in range(1, 4)] + [at_y(d) for d in range(1, 4)] + [sibling]
    for dev in partners:
        pl.semaphore_signal(barrier, inc=1, device_id=dev, device_id_type=MESH)

    xf[...] = in_ref[...].astype(F32)
    scol[0, 0] = xf[:, 31, :].astype(BF)
    scol[0, 1] = xf[:, 0, :].astype(BF)
    code = btgt_ref[...] * 128 + brow_ref[...] * 32 + bcol_ref[...]
    tab[0] = jnp.broadcast_to(code, (16, 128))
    for buf in (xc3, xh3, d23, d13):
        buf[...] = jnp.zeros_like(buf)
    acc[...] = jnp.zeros_like(acc)
    xp[pl.ds(32, PX), :] = in_ref[...].reshape(PX, CH)

    pl.semaphore_wait(barrier, len(partners))

    def halo_send(t, img):
        base = K_HALO + 8 * t
        for i, d in enumerate(halo_dirs):
            if i < 2:
                send(img.at[15 if i == 0 else 0], hrow.at[t, i], base + i, near(*d))
            else:
                send(scol.at[t, 0 if i < 5 else 1], hcol.at[t, i - 2], base + i, near(*d))

    def halo_recv(t):
        base = K_HALO + 8 * t
        for i in range(8):
            got(base + i)
        above, below = row > 0, row < NROW - 1
        left, right = me > 0, me < NZ - 1

        def part(ok, v):
            return jnp.where(ok, v, jnp.zeros_like(v))

        xp[pl.ds(0, 32), :] = part(above, hrow[t, 0])
        xp[pl.ds(544, 32), :] = part(below, hrow[t, 1])
        for side, ok, dst in ((0, left, hl), (3, right, hr)):
            dst[0:1, :] = part(ok & above, hcol[t, side].astype(F32)[15:16, :])
            dst[1:17, :] = part(ok, hcol[t, side + 1].astype(F32))
            dst[17:18, :] = part(ok & below, hcol[t, side + 2].astype(F32)[0:1, :])

        lanes = lax.broadcasted_iota(jnp.int32, (32, CH), 0)

        def one(r, carry):
            at = pl.multiple_of(r * 32, 32)
            mid = xp[pl.ds(at, 32), :]
            c = mid.astype(F32)
            lf = jnp.where(lanes == 0, hl[pl.ds(r, 1), :], pltpu.roll(c, 1, 0))
            rt = jnp.where(lanes == 31, hr[pl.ds(r, 1), :], pltpu.roll(c, 31, 0))
            x3m[pl.ds(at, 32), 0:CH] = lf.astype(BF)
            x3m[pl.ds(at, 32), CH:2 * CH] = mid
            x3m[pl.ds(at, 32), 2 * CH:3 * CH] = rt.astype(BF)
            return carry

        lax.fori_loop(0, 18, one, 0)

    def conv_map(w, j):
        total = mm(x3m[pl.ds(j * HALF, HALF), :], w[0])
        total += mm(x3m[pl.ds(j * HALF + 32, HALF), :], w[1])
        total += mm(x3m[pl.ds(j * HALF + 64, HALF), :], w[2])
        return total

    def turn(src, dst):
        def one(a, carry):
            for b in range(3):
                dst[a, b * CH:(b + 1) * CH, :] = src[2 - a, (2 - b) * CH:(3 - b) * CH, :].T
            return carry

        lax.fori_loop(0, 3, one, 0)

    halo_send(0, in_ref)
    for d in range(1, NZ):
        send(tab.at[0], tab.at[d], K_TAB + d - 1, at_z(d))
    turn(w2_ref, w2t)
    halo_recv(0)

    def ag_key(right, s, j):
        return K_AG + (0 if right else 7) + (s * 2 + j if s < 3 else 6)

    def ag_send(right, s, j):
        src = feats.at[s if right else (NZ - s) % NZ, pl.ds(j * HALF, HALF), :]
        dst = feats.at[s + 1 if right else NZ - 1 - s, pl.ds(j * HALF, HALF), :]
        send(src, dst, ag_key(right, s, j), at_z(1 if right else -1))

    for j in range(2):
        pre = conv_map(tw_ref, j)
        feats[0, pl.ds(j * HALF, HALF), :] = (pre * jax.nn.sigmoid(pre)).astype(BF)
        slope_map[pl.ds(j * HALF, HALF), :] = silu_slope(pre)
        ag_send(True, 0, j)
        ag_send(False, 0, j)

    for d in range(1, NZ):
        got(K_TAB + d - 1)
    for h in range(4):
        base = jnp.zeros((1, 128), jnp.int32)
        for s in range(NZ):
            tile = lax.rem(me - s + NZ, NZ)
            word = tab[s]
            hit = (word >> 7) == me * 4 + h
            value = (word & 127) + tile * PX
            base += jnp.sum(jnp.where(hit, value, 0), axis=0, keepdims=True)
        p = lax.broadcasted_iota(jnp.int32, (POS, 128), 0)
        i, j = p >> 4, p & 15
        ok = (i >= 1) & (i <= 14) & (j < 14)
        gcol[h] = jnp.where(ok, base + (i - 1) * 32 + j, -1)
        p = lax.broadcasted_iota(jnp.int32, (1, POS), 1)
        i, j = p >> 4, p & 15
        ok = (i >= 1) & (i <= 14) & (j < 14)
        both = jnp.concatenate([base, base], axis=1)
        grow[0:1, h * POS:(h + 1) * POS] = jnp.where(ok, both + (i - 1) * 32 + j, -1)

    def take(s, j):
        tile = lax.rem(me - s + NZ, NZ)
        first = tile * PX + j * HALF

        def one(h, carry):
            q = lax.broadcasted_iota(jnp.int32, (POS, 128), 1) + first
            g = gcol[h]
            hot = jnp.concatenate(
                [jnp.where(g == q, 1.0, 0.0), jnp.where(g == q + 128, 1.0, 0.0)], axis=1
            ).astype(BF)
            acc[h] += mm(hot, feats[s, pl.ds(j * HALF, HALF), :])
            return carry

        lax.fori_loop(0, 4, one, 0)

    take(0, 0)
    take(0, 1)
    for s in range(1, 4):
        for j in range(2):
            got(ag_key(True, s - 1, j))
            if s < 3 or j == 0:
                ag_send(True, s, j)
            got(ag_key(False, s - 1, j))
            if s < 3 or j == 1:
                ag_send(False, s, j)
            take(s, j)
            take(NZ - s, j)
            if s == 1 and j == 0:
                turn(w1_ref, w1t)
            if s == 1 and j == 1:
                turn(tw_ref, twt)
    got(ag_key(True, 3, 0))
    take(4, 0)
    got(ag_key(False, 3, 1))
    take(4, 1)

    inside = (lax.broadcasted_iota(jnp.int32, (224, CH), 0) & 15) < 14

    def put(buf, h, value):
        at = pl.multiple_of(h * POS + 32, 16)
        mid = value.astype(BF)
        full = mid.astype(F32)
        buf[pl.ds(at, 224), 0:CH] = pltpu.roll(full, 1, 0).astype(BF)
        buf[pl.ds(at, 224), CH:2 * CH] = mid
        buf[pl.ds(at, 224), 2 * CH:3 * CH] = pltpu.roll(full, 223, 0).astype(BF)

    def conv_box(buf, w, h):
        at = pl.multiple_of(h * POS + 16, 16)
        total = mm(buf[pl.ds(at, 224), :], w[0])
        total += mm(buf[pl.ds(at + 16, 224), :], w[1])
        total += mm(buf[pl.ds(at + 32, 224), :], w[2])
        return total

    def cut(v):
        return jnp.where(inside, v, 0.0)

    def chain(h, carry):
        put(xc3, h, acc[h, 16:240, :])
        pre_one = conv_box(xc3, w1_ref, h)
        put(xh3, h, cut(pre_one * jax.nn.sigmoid(pre_one)))
        slope1[h] = silu_slope(pre_one)
        pre_two = conv_box(xh3, w2_ref, h)
        cotp[:, 0:14, :] = cot_ref[h, 0].astype(F32)
        cotp[:, 14:16, :] = jnp.zeros((14, 2, CH), F32)
        put(d23, h, cut(cotp[...].reshape(224, CH) * silu_slope(pre_two)))
        put(d13, h, cut(conv_box(d23, w2t, h) * slope1[h]))
        at = pl.multiple_of(h * POS, 16)
        bg[pl.ds(at, 16), :] = jnp.zeros((16, CH), BF)
        bg[pl.ds(at + 240, 16), :] = jnp.zeros((16, CH), BF)
        bg[pl.ds(at + 16, 224), :] = conv_box(d13, w1t, h).astype(BF)
        return carry

    lax.fori_loop(0, 4, chain, 0)

    def term(d, j):
        tile = lax.rem(me + d + NZ, NZ)
        q = lax.broadcasted_iota(jnp.int32, (HALF, 4 * POS), 0) + (tile * PX + j * HALF)
        hot = jnp.where(q == grow[0:1, :], 1.0, 0.0).astype(BF)
        return mm(hot, bg[...])

    def rs_item(right, k):
        if k == 0:
            d, j = 4, 0
        else:
            d = 3 - (k - 1) // 2
            j = 1 if k % 2 == 1 else 0
        return d, (j if right else 1 - j)

    def rs_key(right, k):
        return K_RS + (0 if right else 7) + k

    def rs_step(k):
        for right in (True, False):
            d, j = rs_item(right, k)
            side = 0 if right else 1
            value = term(d if right else -d, j)
            if k >= 2:
                got(rs_key(right, k - 2))
                value += rs_r[side, k - 2].astype(F32)
            rs_s[side, k] = value.astype(BF)
            send(rs_s.at[side, k], rs_r.at[side, k], rs_key(right, k), at_z(1 if right else -1))

    def wgrad(g, buf, dbuf):
        for h in range(4):
            xt[:, h * POS:(h + 1) * POS] = buf[16 + h * POS:16 + (h + 1) * POS, CH:2 * CH].T

        def one(a, carry):
            at = pl.multiple_of(32 - a * 16, 16)
            for b in range(3):
                value = mm(xt[...], dbuf[pl.ds(at, 4 * POS), (2 - b) * CH:(3 - b) * CH])
                low, high = value[:, 0:128], value[:, 128:256]
                own[g, a * 3 + b] = jnp.where(core == 0, low, high)
                snd[g, a * 3 + b] = jnp.where(core == 0, high, low).astype(BF)
            return carry

        lax.fori_loop(0, 3, one, 0)
        send(snd.at[g], rc.at[g], K_AR + g * AR_N, sibling)

    def axes(g):
        if g == 0:
            return at_x, px, NX, at_y, py, NY
        return at_y, py, NY, at_x, px, NX

    def ar1(g):
        k = K_AR + g * AR_N
        at1, p1, n1 = axes(g)[:3]
        got(k)

        def one(t, carry):
            v = own[g, t] + rc[g, t].astype(F32)
            own[g, t] = v
            s1[g, t] = v.astype(BF)
            return carry

        lax.fori_loop(0, 9, one, 0)
        for d in range(1, 4):
            q = lax.rem(p1 + d, n1)
            send(s1.at[g, :, pl.ds(q * 64, 64), :], r1.at[g, d - 1], k + d, at1(d))

    def ar2(g):
        k = K_AR + g * AR_N
        at1, p1, n1, at2, p2, n2 = axes(g)
        for d in range(1, 4):
            got(k + d)

        def one(t, carry):
            v = own[g, t, pl.ds(p1 * 64, 64), :]
            for d in range(3):
                v += r1[g, d, t].astype(F32)
            t2[g, t] = v
            s2[g, t] = v.astype(BF)
            return carry

        lax.fori_loop(0, 9, one, 0)
        for d in range(1, 4):
            q = lax.rem(p2 + d, n2)
            send(s2.at[g, :, pl.ds(q * 16, 16), :], r2.at[g, d - 1], k + 3 + d, at2(d))

    def ar3(g):
        k = K_AR + g * AR_N
        p2 = axes(g)[4]
        for d in range(1, 4):
            got(k + 3 + d)
        v = t2[g, :, pl.ds(p2 * 16, 16), :]
        for d in range(3):
            v += r2[g, d].astype(F32)
        t3[g, 0:9] = v
        t3[g, 9:16] = jnp.zeros((7, 16, 128), F32)
        s3[g, 0:9] = v.astype(BF)
        s3[g, 9:16] = jnp.zeros((7, 16, 128), BF)
        for d in range(1, NZ):
            q = lax.rem(me + d, NZ)
            send(s3.at[g, pl.ds(q * 2, 2)], r3.at[g, d - 1], k + 6 + d, at_z(d))

    def ar4(g):
        k = K_AR + g * AR_N
        for d in range(1, NZ):
            got(k + 6 + d)
        v = t3[g, pl.ds(me * 2, 2)]
        for d in range(NZ - 1):
            v += r3[g, d].astype(F32)
        zb[g, pl.ds(me * 2, 2)] = v.astype(BF)
        for d in range(1, NZ):
            part = zb.at[g, pl.ds(me * 2, 2)]
            send(part, part, k + 13 + d, at_z(d))

    def ar5(g):
        k = K_AR + g * AR_N
        at1, p1, n1, at2, p2, n2 = axes(g)
        for d in range(1, NZ):
            got(k + 13 + d)
        at = pl.multiple_of(p1 * 64 + p2 * 16, 16)
        gsum_ref[g, core, :, pl.ds(at, 16), :] = zb[g, 0:9]
        part = gsum_ref.at[g, core, :, pl.ds(at, 16), :]
        for d in range(1, 4):
            send(part, part, k + 20 + d, at2(d))

    def ar6(g):
        k = K_AR + g * AR_N
        at1, p1, n1 = axes(g)[:3]
        for d in range(1, 4):
            got(k + 20 + d)
        part = gsum_ref.at[g, core, :, pl.ds(p1 * 64, 64), :]
        for d in range(1, 4):
            send(part, part, k + 23 + d, at1(d))

    def ar7(g):
        k = K_AR + g * AR_N
        for d in range(1, 4):
            got(k + 23 + d)
        part = gsum_ref.at[g, core]
        send(part, part, k + 27, sibling)

    rs_step(0)
    rs_step(1)
    wgrad(1, xh3, d23)
    rs_step(2)
    wgrad(0, xc3, d13)
    rs_step(3)
    ar1(1)
    ar1(0)
    rs_step(4)
    rs_step(5)
    ar2(1)
    ar2(0)
    rs_step(6)
    ar3(1)
    ar3(0)

    for j in range(2):
        total = term(0, j)
        for right in (True, False):
            k = 6 if rs_item(right, 6)[1] == j else 5
            got(rs_key(right, k))
            total += rs_r[0 if right else 1, k].astype(F32)
        grad = (total * slope_map[pl.ds(j * HALF, HALF), :]).astype(BF)
        xp[pl.ds(32 + j * HALF, HALF), :] = grad
        dm[8 * j:8 * j + 8] = grad.reshape(8, 32, CH)
        xf[8 * j:8 * j + 8] = grad.astype(F32).reshape(8, 32, CH)
    scol[1, 0] = xf[:, 31, :].astype(BF)
    scol[1, 1] = xf[:, 0, :].astype(BF)
    halo_send(1, dm)
    ar4(1)
    ar4(0)
    halo_recv(1)
    ar5(1)
    ar5(0)
    for j in range(2):
        gmap_ref[8 * j:8 * j + 8] = conv_map(twt, j).astype(BF).reshape(8, 32, CH)
    ar6(1)
    ar6(0)
    ar7(1)
    ar7(0)
    got(K_AR + 27)
    got(K_AR + AR_N + 27)
    for k in sorted(live):
        live[k].wait_send()


def step(in_map, tile_w, head_w1, head_w2, box_row, box_col, box_target, head_cot):
    vm = pltpu.VMEM
    scratch = [
        vm((16, 32, CH), F32),
        vm((576, CH), BF),
        vm((576, 3 * CH), BF),
        vm((PX, CH), F32),
        vm((2, 2, 16, CH), BF),
        vm((2, 2, 32, CH), BF),
        vm((2, 6, 16, CH), BF),
        vm((24, CH), F32),
        vm((24, CH), F32),
        vm((NZ, 16, 128), jnp.int32),
        vm((4, POS, 128), jnp.int32),
        vm((1, 4 * POS), jnp.int32),
        vm((NZ, PX, CH), BF),
        vm((4, POS, CH), F32),
        vm((1056, 3 * CH), BF),
        vm((1056, 3 * CH), BF),
        vm((1056, 3 * CH), BF),
        vm((1056, 3 * CH), BF),
        vm((4, 224, CH), F32),
        vm((14, 16, CH), F32),
        vm((CH, 4 * POS), BF),
        vm((3, 3 * CH, CH), BF),
        vm((3, 3 * CH, CH), BF),
        vm((3, 3 * CH, CH), BF),
        vm((4 * POS, CH), BF),
        vm((2, 7, HALF, CH), BF),
        vm((2, 7, HALF, CH), BF),
        vm((16, 32, CH), BF),
        vm((2, 9, 256, 128), F32),
        vm((2, 9, 256, 128), BF),
        vm((2, 9, 256, 128), BF),
        vm((2, 9, 256, 128), BF),
        vm((2, 3, 9, 64, 128), BF),
        vm((2, 9, 64, 128), F32),
        vm((2, 9, 64, 128), BF),
        vm((2, 3, 9, 16, 128), BF),
        vm((2, 16, 16, 128), F32),
        vm((2, 16, 16, 128), BF),
        vm((2, 7, 2, 16, 128), BF),
        vm((2, 16, 16, 128), BF),
        pltpu.SemaphoreType.DMA((N_SEM,)),
        pltpu.SemaphoreType.DMA((N_SEM,)),
    ]
    in_vmem = pl.BlockSpec(memory_space=pltpu.VMEM)
    grad_map, sums = pl.pallas_call(
        kernel,
        out_shape=(
            jax.ShapeDtypeStruct((16, 32, CH), BF),
            jax.ShapeDtypeStruct((2, 2, 9, 256, 128), BF),
        ),
        in_specs=[in_vmem] * 8,
        out_specs=(in_vmem, in_vmem),
        scratch_shapes=scratch,
        compiler_params=pltpu.CompilerParams(
            collective_id=0, has_side_effects=True, vmem_limit_bytes=58 * 1024 * 1024
        ),
        cost_estimate=pl.CostEstimate(flops=8 * 10**9, bytes_accessed=10**7, transcendentals=10**6),
    )(
        in_map,
        tile_w.reshape(3, 3 * CH, CH),
        head_w1.reshape(3, 3 * CH, CH),
        head_w2.reshape(3, 3 * CH, CH),
        box_row,
        box_col,
        box_target,
        head_cot,
    )
    factor = 1.0 / math.sqrt(32 * 8 * 4 * 14 * 14)
    sums = sums.transpose(0, 2, 3, 1, 4).astype(F32) * factor
    sums = sums.reshape(2, 3, 3, CH, CH)
    return grad_map, sums[0], sums[1]


def solution(mesh):
    in_specs = (
        P("row", "col", None),
        P(),
        P(),
        P(),
        P("row", "col"),
        P("row", "col"),
        P("row", "col"),
        P("row", "col", None, None, None),
    )
    out_specs = (P("row", "col", None), P(), P())
    return jax.shard_map(step, mesh=mesh, in_specs=in_specs, out_specs=out_specs, check_vma=False)
```

```python
import math

import jax
import jax.numpy as jnp
from jax import lax
from jax.experimental import pallas as pl
from jax.experimental.pallas import tpu as pltpu
from jax.sharding import PartitionSpec as P

MESH = pl.DeviceIdType.MESH
BF = jnp.bfloat16
F32 = jnp.float32
NZ = 8
NX = 4
NY = 4
NROW = 32
PX = 512
HALF = 256
POS = 256
CH = 256
K_HALO = 0
K_TAB = 16
K_AG = 23
K_RS = 37
K_AR = 51
AR_N = 28
N_SEM = K_AR + 4 * AR_N
PARTS = ((1, 0, 5, False), (1, 5, 4, True), (0, 0, 5, True), (0, 5, 4, False))


def silu_slope(values):
    sigma = jax.nn.sigmoid(values)
    return sigma * (1.0 + values * (1.0 - sigma))


def mm(a, b):
    return jnp.dot(a, b, preferred_element_type=F32)


def kernel(
    in_ref, tw_ref, w1_ref, w2_ref, brow_ref, bcol_ref, btgt_ref, cot_ref,
    gmap_ref, gsum_ref,
    xf, xp, x3m, slope_map, scol, hrow, hcol, hl, hr,
    tab, gcol, grow, feats, acc, xc3, xh3, d23, d13, slope1, cotf, cots, xt,
    twt, w1t, w2t, bg, rs_s, rs_r, dm,
    own, snd, rc, s1, r1, t2, s2, r2, t3, s3, r3, zb,
    ssem, rsem,
):
    row = lax.axis_index("row")
    me = lax.axis_index("col")
    px = row // 8
    py = lax.rem(row // 2, NY)
    core = lax.rem(row, 2)

    def at_x(d):
        return (lax.rem(px + d, NX) * 8 + py * 2 + core, me)

    def at_y(d):
        return (px * 8 + lax.rem(py + d, NY) * 2 + core, me)

    def at_z(d):
        return (row, lax.rem(me + d + NZ, NZ))

    sibling = (row + 1 - 2 * core, me)

    def near(dr, dc):
        return (lax.rem(row + dr + NROW, NROW), lax.rem(me + dc + NZ, NZ))

    live = {}

    def send(src, dst, k, dev):
        copy = pltpu.make_async_remote_copy(
            src_ref=src, dst_ref=dst, send_sem=ssem.at[k], recv_sem=rsem.at[k],
            device_id=dev, device_id_type=MESH,
        )
        copy.start()
        live[k] = copy

    def got(k):
        live[k].wait_recv()

    halo_dirs = [(1, 0), (-1, 0), (1, 1), (0, 1), (-1, 1), (1, -1), (0, -1), (-1, -1)]

    barrier = pltpu.get_barrier_semaphore()
    partners = [near(*d) for d in halo_dirs]
    partners += [at_z(d) for d in range(2, 7)]
    partners += [at_x(d) for d in range(1, 4)] + [at_y(d) for d in range(1, 4)] + [sibling]
    for dev in partners:
        pl.semaphore_signal(barrier, inc=1, device_id=dev, device_id_type=MESH)

    xf[...] = in_ref[...].astype(F32)
    scol[0, 0] = xf[:, 31, :].astype(BF)
    scol[0, 1] = xf[:, 0, :].astype(BF)
    tab[0] = jnp.full((8, 128), -128, jnp.int32)
    tab[0, 0:1, 0:16] = btgt_ref[...] * 128 + brow_ref[...] * 32 + bcol_ref[...]
    for buf in (xc3, xh3, d23, d13):
        for h in range(5):
            at = max(h * POS, 0)
            buf[at:at + 32, :] = jnp.zeros((32, 3 * CH), BF)
    acc[...] = jnp.zeros_like(acc)
    xp[pl.ds(32, PX), :] = in_ref[...].reshape(PX, CH)

    pl.semaphore_wait(barrier, len(partners))

    def halo_send(t, img):
        base = K_HALO + 8 * t
        for i, d in enumerate(halo_dirs):
            if i < 2:
                send(img.at[15 if i == 0 else 0], hrow.at[t, i], base + i, near(*d))
            else:
                send(scol.at[t, 0 if i < 5 else 1], hcol.at[t, i - 2], base + i, near(*d))

    def halo_recv(t):
        base = K_HALO + 8 * t
        for i in range(8):
            got(base + i)
        above, below = row > 0, row < NROW - 1
        left, right = me > 0, me < NZ - 1

        def part(ok, v):
            return jnp.where(ok, v, jnp.zeros_like(v))

        xp[pl.ds(0, 32), :] = part(above, hrow[t, 0])
        xp[pl.ds(544, 32), :] = part(below, hrow[t, 1])
        for side, ok, dst in ((0, left, hl), (3, right, hr)):
            dst[0:1, :] = part(ok & above, hcol[t, side].astype(F32)[15:16, :])
            dst[1:17, :] = part(ok, hcol[t, side + 1].astype(F32))
            dst[17:18, :] = part(ok & below, hcol[t, side + 2].astype(F32)[0:1, :])

        lanes = lax.broadcasted_iota(jnp.int32, (32, CH), 0)

        def one(r, carry):
            at = pl.multiple_of(r * 32, 32)
            mid = xp[pl.ds(at, 32), :]
            c = mid.astype(F32)
            lf = jnp.where(lanes == 0, hl[pl.ds(r, 1), :], pltpu.roll(c, 1, 0))
            rt = jnp.where(lanes == 31, hr[pl.ds(r, 1), :], pltpu.roll(c, 31, 0))
            x3m[pl.ds(at, 32), 0:CH] = lf.astype(BF)
            x3m[pl.ds(at, 32), CH:2 * CH] = mid
            x3m[pl.ds(at, 32), 2 * CH:3 * CH] = rt.astype(BF)
            return carry

        lax.fori_loop(0, 18, one, 0)

    def conv_map(w, j):
        total = mm(x3m[pl.ds(j * HALF, HALF), :], w[0])
        total += mm(x3m[pl.ds(j * HALF + 32, HALF), :], w[1])
        total += mm(x3m[pl.ds(j * HALF + 64, HALF), :], w[2])
        return total

    def turn(src, dst, taps):
        for a in taps:
            for b in range(3):
                dst[a, b * CH:(b + 1) * CH, :] = src[2 - a, (2 - b) * CH:(3 - b) * CH, :].T

    halo_send(0, in_ref)
    for d in range(1, NZ):
        send(tab.at[0], tab.at[d], K_TAB + d - 1, at_z(d))
    turn(w2_ref, w2t, (0, 1, 2))
    halo_recv(0)

    def ag_key(right, s, j):
        return K_AG + (0 if right else 7) + (s * 2 + j if s < 3 else 6)

    def ag_send(right, s, j):
        src = feats.at[s if right else (NZ - s) % NZ, pl.ds(j * HALF, HALF), :]
        dst = feats.at[s + 1 if right else NZ - 1 - s, pl.ds(j * HALF, HALF), :]
        send(src, dst, ag_key(right, s, j), at_z(1 if right else -1))

    for j in range(2):
        pre = conv_map(tw_ref, j)
        feats[0, pl.ds(j * HALF, HALF), :] = (pre * jax.nn.sigmoid(pre)).astype(BF)
        slope_map[pl.ds(j * HALF, HALF), :] = silu_slope(pre)
        ag_send(True, 0, j)
        ag_send(False, 0, j)

    for d in range(1, NZ):
        got(K_TAB + d - 1)
    for h in range(4):
        base = jnp.zeros((1, 1), jnp.int32)
        for s in range(NZ):
            tile = lax.rem(me - s + NZ, NZ)
            word = tab[s, 0:1, :]
            hit = (word >> 7) == me * 4 + h
            value = (word & 127) + tile * PX
            base += jnp.sum(jnp.where(hit, value, 0), axis=1, keepdims=True)
        p = lax.broadcasted_iota(jnp.int32, (POS, 128), 0)
        i, j = p >> 4, p & 15
        ok = (i >= 1) & (i <= 14) & (j < 14)
        gcol[h] = jnp.where(ok, base + (i - 1) * 32 + j, -1)
        p = lax.broadcasted_iota(jnp.int32, (1, POS), 1)
        i, j = p >> 4, p & 15
        ok = (i >= 1) & (i <= 14) & (j < 14)
        grow[0:1, h * POS:(h + 1) * POS] = jnp.where(ok, base + (i - 1) * 32 + j, -1)

    def take(s, j):
        tile = lax.rem(me - s + NZ, NZ)
        first = tile * PX + j * HALF

        def one(h, carry):
            q = lax.broadcasted_iota(jnp.int32, (POS, 128), 1) + first
            g = gcol[h]
            hot = jnp.concatenate(
                [jnp.where(g == q, 1.0, 0.0), jnp.where(g == q + 128, 1.0, 0.0)], axis=1
            ).astype(BF)
            acc[h] += mm(hot, feats[s, pl.ds(j * HALF, HALF), :])
            return carry

        lax.fori_loop(0, 4, one, 0)

    take(0, 0)
    take(0, 1)

    def spread(i, carry):
        cotf[...] = cot_ref[i].astype(F32)
        for h in range(4):
            cots[h, i, 0:14, :] = cotf[:, h, :]
            cots[h, i, 14:16, :] = jnp.zeros((2, CH), F32)
        return carry

    lax.fori_loop(0, 14, spread, 0)
    for s in range(1, 4):
        for j in range(2):
            got(ag_key(True, s - 1, j))
            if s < 3 or j == 0:
                ag_send(True, s, j)
            got(ag_key(False, s - 1, j))
            if s < 3 or j == 1:
                ag_send(False, s, j)
            take(s, j)
            take(NZ - s, j)
            if s < 3:
                n = 2 * (s - 1) + j
                if n < 3:
                    turn(w1_ref, w1t, (n,))
                turn(tw_ref, twt, (n,) if n < 3 else ())
    got(ag_key(True, 3, 0))
    take(4, 0)
    got(ag_key(False, 3, 1))
    take(4, 1)

    inside = (lax.broadcasted_iota(jnp.int32, (224, CH), 0) & 15) < 14

    def put(buf, h, value):
        at = h * POS + 32
        mid = value.astype(BF)
        full = mid.astype(F32)
        buf[pl.ds(at, 224), 0:CH] = pltpu.roll(full, 1, 0).astype(BF)
        buf[pl.ds(at, 224), CH:2 * CH] = mid
        buf[pl.ds(at, 224), 2 * CH:3 * CH] = pltpu.roll(full, 223, 0).astype(BF)

    def conv_box(buf, w, h):
        at = h * POS + 16
        total = mm(buf[pl.ds(at, 224), :], w[0])
        total += mm(buf[pl.ds(at + 16, 224), :], w[1])
        total += mm(buf[pl.ds(at + 32, 224), :], w[2])
        return total

    def cut(v):
        return jnp.where(inside, v, 0.0)

    for h in range(4):
        put(xc3, h, acc[h, 16:240, :])
    for h in range(4):
        pre = conv_box(xc3, w1_ref, h)
        put(xh3, h, cut(pre * jax.nn.sigmoid(pre)))
        slope1[h] = silu_slope(pre)
    for h in range(4):
        pre = conv_box(xh3, w2_ref, h)
        put(d23, h, cut(cots[h].reshape(224, CH) * silu_slope(pre)))

    def term(d, j):
        tile = lax.rem(me + d + NZ, NZ)
        q = lax.broadcasted_iota(jnp.int32, (HALF, 4 * POS), 0) + (tile * PX + j * HALF)
        hot = jnp.where(q == grow[0:1, :], 1.0, 0.0).astype(BF)
        return mm(hot, bg[...])

    def rs_item(right, k):
        if k == 0:
            d, j = 4, 0
        else:
            d = 3 - (k - 1) // 2
            j = 1 if k % 2 == 1 else 0
        return d, (j if right else 1 - j)

    def rs_key(right, k):
        return K_RS + (0 if right else 7) + k

    def rs_step(k):
        for right in (True, False):
            d, j = rs_item(right, k)
            side = 0 if right else 1
            value = term(d if right else -d, j)
            if k >= 2:
                got(rs_key(right, k - 2))
                value += rs_r[side, k - 2].astype(F32)
            rs_s[side, k] = value.astype(BF)
            send(rs_s.at[side, k], rs_r.at[side, k], rs_key(right, k), at_z(1 if right else -1))

    def wgrad(g, buf, dbuf):
        for h in range(4):
            xt[:, h * POS:(h + 1) * POS] = buf[16 + h * POS:16 + (h + 1) * POS, CH:2 * CH].T

        def one(a, carry):
            at = pl.multiple_of(32 - a * 16, 16)
            for b in range(3):
                value = mm(xt[...], dbuf[pl.ds(at, 4 * POS), (2 - b) * CH:(3 - b) * CH])
                low, high = value[:, 0:128], value[:, 128:256]
                own[g, a * 3 + b] = jnp.where(core == 0, low, high)
                snd[g, a * 3 + b] = jnp.where(core == 0, high, low).astype(BF)
            return carry

        lax.fori_loop(0, 3, one, 0)
        for n in (2 * (1 - g), 2 * (1 - g) + 1):
            t0, nt = PARTS[n][1:3]
            span = pl.ds(t0, nt)
            send(snd.at[g, span], rc.at[g, span], K_AR + n * AR_N, sibling)

    def axes(n):
        if PARTS[n][3]:
            return at_x, px, NX, at_y, py, NY
        return at_y, py, NY, at_x, px, NX

    def ar1(n):
        g, t0, nt, _ = PARTS[n]
        k = K_AR + n * AR_N
        at1, p1, n1 = axes(n)[:3]
        got(k)

        def one(t, carry):
            v = own[g, t] + rc[g, t].astype(F32)
            own[g, t] = v
            s1[g, t] = v.astype(BF)
            return carry

        lax.fori_loop(t0, t0 + nt, one, 0)
        for d in range(1, 4):
            q = lax.rem(p1 + d, n1)
            src = s1.at[g, pl.ds(t0, nt), pl.ds(q * 64, 64), :]
            send(src, r1.at[n, d - 1, pl.ds(0, nt)], k + d, at1(d))

    def ar2(n):
        g, t0, nt, _ = PARTS[n]
        k = K_AR + n * AR_N
        at1, p1, n1, at2, p2, n2 = axes(n)
        for d in range(1, 4):
            got(k + d)

        def one(t, carry):
            v = own[g, t0 + t, pl.ds(p1 * 64, 64), :]
            for d in range(3):
                v += r1[n, d, t].astype(F32)
            t2[n, t] = v
            s2[n, t] = v.astype(BF)
            return carry

        lax.fori_loop(0, nt, one, 0)
        for d in range(1, 4):
            q = lax.rem(p2 + d, n2)
            src = s2.at[n, pl.ds(0, nt), pl.ds(q * 16, 16), :]
            send(src, r2.at[n, d - 1, pl.ds(0, nt)], k + 3 + d, at2(d))

    def ar3(n):
        nt = PARTS[n][2]
        k = K_AR + n * AR_N
        p2 = axes(n)[4]
        for d in range(1, 4):
            got(k + 3 + d)
        v = t2[n, 0:nt, pl.ds(p2 * 16, 16), :]
        for d in range(3):
            v += r2[n, d, 0:nt].astype(F32)
        t3[n, 0:nt] = v
        t3[n, nt:8] = jnp.zeros((8 - nt, 16, 128), F32)
        s3[n, 0:nt] = v.astype(BF)
        s3[n, nt:8] = jnp.zeros((8 - nt, 16, 128), BF)
        for d in range(1, NZ):
            q = lax.rem(me + d, NZ)
            send(s3.at[n, q], r3.at[n, d - 1], k + 6 + d, at_z(d))

    def ar4(n):
        k = K_AR + n * AR_N
        for d in range(1, NZ):
            got(k + 6 + d)
        v = t3[n, me]
        for d in range(NZ - 1):
            v += r3[n, d].astype(F32)
        zb[n, me] = v.astype(BF)
        for d in range(1, NZ):
            send(zb.at[n, me], zb.at[n, me], k + 13 + d, at_z(d))

    def ar5(n):
        g, t0, nt, _ = PARTS[n]
        k = K_AR + n * AR_N
        at1, p1, n1, at2, p2, n2 = axes(n)
        for d in range(1, NZ):
            got(k + 13 + d)
        at = pl.multiple_of(p1 * 64 + p2 * 16, 16)
        gsum_ref[g, core, t0:t0 + nt, pl.ds(at, 16), :] = zb[n, 0:nt]
        part = gsum_ref.at[g, core, pl.ds(t0, nt), pl.ds(at, 16), :]
        for d in range(1, 4):
            send(part, part, k + 20 + d, at2(d))

    def ar6(n):
        g, t0, nt, _ = PARTS[n]
        k = K_AR + n * AR_N
        at1, p1, n1 = axes(n)[:3]
        for d in range(1, 4):
            got(k + 20 + d)
        part = gsum_ref.at[g, core, pl.ds(t0, nt), pl.ds(p1 * 64, 64), :]
        for d in range(1, 4):
            send(part, part, k + 23 + d, at1(d))

    def ar7(n):
        g, t0, nt, _ = PARTS[n]
        k = K_AR + n * AR_N
        for d in range(1, 4):
            got(k + 23 + d)
        part = gsum_ref.at[g, core, pl.ds(t0, nt)]
        send(part, part, k + 27, sibling)

    def both(stage, g):
        stage(2 * (1 - g))
        stage(2 * (1 - g) + 1)

    wgrad(1, xh3, d23)
    for h in range(4):
        put(d13, h, cut(conv_box(d23, w2t, h) * slope1[h]))
    for h in range(4):
        bg[h * POS:h * POS + 16, :] = jnp.zeros((16, CH), BF)
        bg[h * POS + 240:(h + 1) * POS, :] = jnp.zeros((16, CH), BF)
        bg[h * POS + 16:h * POS + 240, :] = conv_box(d13, w1t, h).astype(BF)
    rs_step(0)
    both(ar1, 1)
    rs_step(1)
    wgrad(0, xc3, d13)
    rs_step(2)
    both(ar1, 0)
    rs_step(3)
    both(ar2, 1)
    rs_step(4)
    both(ar2, 0)
    both(ar3, 1)
    rs_step(5)
    both(ar3, 0)
    both(ar4, 1)
    rs_step(6)
    both(ar4, 0)
    both(ar5, 1)

    for j in range(2):
        total = term(0, j)
        for right in (True, False):
            k = 6 if rs_item(right, 6)[1] == j else 5
            got(rs_key(right, k))
            total += rs_r[0 if right else 1, k].astype(F32)
        grad = (total * slope_map[pl.ds(j * HALF, HALF), :]).astype(BF)
        xp[pl.ds(32 + j * HALF, HALF), :] = grad
        dm[8 * j:8 * j + 8] = grad.reshape(8, 32, CH)
        xf[8 * j:8 * j + 8] = grad.astype(F32).reshape(8, 32, CH)
    scol[1, 0] = xf[:, 31, :].astype(BF)
    scol[1, 1] = xf[:, 0, :].astype(BF)
    halo_send(1, dm)
    both(ar5, 0)
    both(ar6, 1)
    halo_recv(1)
    for j in range(2):
        gmap_ref[8 * j:8 * j + 8] = conv_map(twt, j).astype(BF).reshape(8, 32, CH)
    both(ar6, 0)
    both(ar7, 1)
    both(ar7, 0)
    for n in range(4):
        got(K_AR + n * AR_N + 27)
    for k in sorted(live):
        live[k].wait_send()


def finish(map_ref, sums_ref, out_ref, first_ref, second_ref):
    factor = 1.0 / math.sqrt(32 * 8 * 4 * 14 * 14)
    out_ref[...] = map_ref[...]
    for g, ref in enumerate((first_ref, second_ref)):
        for half in range(2):
            ref[:, :, half * 128:half * 128 + 128] = sums_ref[g, half].astype(F32) * factor


def step(in_map, tile_w, head_w1, head_w2, box_row, box_col, box_target, head_cot):
    vm = pltpu.VMEM
    scratch = [
        vm((16, 32, CH), F32),
        vm((576, CH), BF),
        vm((576, 3 * CH), BF),
        vm((PX, CH), F32),
        vm((2, 2, 16, CH), BF),
        vm((2, 2, 32, CH), BF),
        vm((2, 6, 16, CH), BF),
        vm((24, CH), F32),
        vm((24, CH), F32),
        vm((NZ, 8, 128), jnp.int32),
        vm((4, POS, 128), jnp.int32),
        vm((1, 4 * POS), jnp.int32),
        vm((NZ, PX, CH), BF),
        vm((4, POS, CH), F32),
        vm((1056, 3 * CH), BF),
        vm((1056, 3 * CH), BF),
        vm((1056, 3 * CH), BF),
        vm((1056, 3 * CH), BF),
        vm((4, 224, CH), F32),
        vm((14, 4, CH), F32),
        vm((4, 14, 16, CH), F32),
        vm((CH, 4 * POS), BF),
        vm((3, 3 * CH, CH), BF),
        vm((3, 3 * CH, CH), BF),
        vm((3, 3 * CH, CH), BF),
        vm((4 * POS, CH), BF),
        vm((2, 7, HALF, CH), BF),
        vm((2, 7, HALF, CH), BF),
        vm((16, 32, CH), BF),
        vm((2, 9, 256, 128), F32),
        vm((2, 9, 256, 128), BF),
        vm((2, 9, 256, 128), BF),
        vm((2, 9, 256, 128), BF),
        vm((4, 3, 5, 64, 128), BF),
        vm((4, 5, 64, 128), F32),
        vm((4, 5, 64, 128), BF),
        vm((4, 3, 5, 16, 128), BF),
        vm((4, NZ, 16, 128), F32),
        vm((4, NZ, 16, 128), BF),
        vm((4, 7, 16, 128), BF),
        vm((4, NZ, 16, 128), BF),
        pltpu.SemaphoreType.DMA((N_SEM,)),
        pltpu.SemaphoreType.DMA((N_SEM,)),
    ]
    in_vmem = pl.BlockSpec(memory_space=pltpu.VMEM)
    grad_map, sums = pl.pallas_call(
        kernel,
        out_shape=(
            jax.ShapeDtypeStruct((16, 32, CH), BF),
            jax.ShapeDtypeStruct((2, 2, 9, 256, 128), BF),
        ),
        in_specs=[in_vmem] * 8,
        out_specs=(in_vmem, in_vmem),
        scratch_shapes=scratch,
        compiler_params=pltpu.CompilerParams(
            collective_id=0, has_side_effects=True, vmem_limit_bytes=58 * 1024 * 1024
        ),
        cost_estimate=pl.CostEstimate(flops=8 * 10**9, bytes_accessed=10**7, transcendentals=10**6),
    )(
        in_map,
        tile_w.reshape(3, 3 * CH, CH),
        head_w1.reshape(3, 3 * CH, CH),
        head_w2.reshape(3, 3 * CH, CH),
        box_row.T,
        box_col.T,
        box_target.T,
        head_cot[:, 0].transpose(1, 2, 0, 3),
    )
    grad_map, first, second = pl.pallas_call(
        finish,
        grid=(3,),
        out_shape=(
            jax.ShapeDtypeStruct((16, 32, CH), BF),
            jax.ShapeDtypeStruct((9, CH, CH), F32),
            jax.ShapeDtypeStruct((9, CH, CH), F32),
        ),
        in_specs=[
            pl.BlockSpec((16, 32, CH), lambda i: (0, 0, 0)),
            pl.BlockSpec((2, 2, 3, CH, 128), lambda i: (0, 0, i, 0, 0)),
        ],
        out_specs=(
            pl.BlockSpec((16, 32, CH), lambda i: (0, 0, 0)),
            pl.BlockSpec((3, CH, CH), lambda i: (i, 0, 0)),
            pl.BlockSpec((3, CH, CH), lambda i: (i, 0, 0)),
        ),
    )(grad_map, sums)
    return grad_map, first.reshape(3, 3, CH, CH), second.reshape(3, 3, CH, CH)


def solution(mesh):
    in_specs = (
        P("row", "col", None),
        P(),
        P(),
        P(),
        P("row", "col"),
        P("row", "col"),
        P("row", "col"),
        P("row", "col", None, None, None),
    )
    out_specs = (P("row", "col", None), P(), P())
    return jax.shard_map(step, mesh=mesh, in_specs=in_specs, out_specs=out_specs, check_vma=False)
```

```python
import math

import jax
import jax.numpy as jnp
from jax import lax
from jax.experimental import pallas as pl
from jax.experimental.pallas import tpu as pltpu
from jax.sharding import PartitionSpec as P

MESH = pl.DeviceIdType.MESH
BF = jnp.bfloat16
F32 = jnp.float32
NZ = 8
NX = 4
NY = 4
NROW = 32
PX = 512
HALF = 256
POS = 256
CH = 256
K_HALO = 0
K_TAB = 16
K_AG = 23
K_RS = 37
K_AR = 51
AR_N = 33
N_SEM = K_AR + 4 * AR_N
PARTS = ((1, 0, 5, False), (1, 5, 4, True), (0, 0, 5, True), (0, 5, 4, False))


def silu_slope(values):
    sigma = jax.nn.sigmoid(values)
    return sigma * (1.0 + values * (1.0 - sigma))


def mm(a, b):
    return jnp.dot(a, b, preferred_element_type=F32)


def kernel(
    in_ref, tw_any, w1_any, w2_any, brow_ref, bcol_ref, btgt_ref, cot_any,
    gmap_ref, gsum_ref,
    tw_ref, w1_ref, w2_ref, cot_ref, xf, xp, x3m, slope_map, scol, hrow, hcol, hl, hr,
    tab, gcol, grow, feats, acc, xc3, xh3, d23, d13, slope1, cotf, cots, xt,
    twt, w1t, w2t, bg, rs_s, rs_r, dm,
    own, snd, rc, s1, r1, t2, s2, r2, t3, s3, r3, zb,
    ssem, rsem, lsem,
):
    row = lax.axis_index("row")
    me = lax.axis_index("col")
    px = row // 8
    py = lax.rem(row // 2, NY)
    core = lax.rem(row, 2)

    def at_x(d):
        return (lax.rem(px + d, NX) * 8 + py * 2 + core, me)

    def at_y(d):
        return (px * 8 + lax.rem(py + d, NY) * 2 + core, me)

    def at_z(d):
        return (row, lax.rem(me + d + NZ, NZ))

    sibling = (row + 1 - 2 * core, me)

    def near(dr, dc):
        return (lax.rem(row + dr + NROW, NROW), lax.rem(me + dc + NZ, NZ))

    live = {}

    def send(src, dst, k, dev):
        copy = pltpu.make_async_remote_copy(
            src_ref=src, dst_ref=dst, send_sem=ssem.at[k], recv_sem=rsem.at[k],
            device_id=dev, device_id_type=MESH,
        )
        copy.start()
        live[k] = copy

    def got(k):
        live[k].wait_recv()

    halo_dirs = [(1, 0), (-1, 0), (1, 1), (0, 1), (-1, 1), (1, -1), (0, -1), (-1, -1)]

    barrier = pltpu.get_barrier_semaphore()
    partners = [near(*d) for d in halo_dirs]
    partners += [at_z(d) for d in range(2, 7)]
    partners += [at_x(d) for d in range(1, 4)] + [at_y(d) for d in range(1, 4)] + [sibling]
    for dev in partners:
        pl.semaphore_signal(barrier, inc=1, device_id=dev, device_id_type=MESH)

    loads = []
    for n, (src, dst) in enumerate(
        ((tw_any, tw_ref), (w2_any, w2_ref), (w1_any, w1_ref), (cot_any, cot_ref))
    ):
        loads.append(pltpu.make_async_copy(src, dst, lsem.at[n]))
        loads[n].start()

    xf[...] = in_ref[...].astype(F32)
    scol[0, 0] = xf[:, 31, :].astype(BF)
    scol[0, 1] = xf[:, 0, :].astype(BF)
    tab[0] = jnp.full((8, 128), -128, jnp.int32)
    tab[0, 0:1, 0:16] = btgt_ref[...] * 128 + brow_ref[...] * 32 + bcol_ref[...]
    xp[pl.ds(32, PX), :] = in_ref[...].reshape(PX, CH)

    pl.semaphore_wait(barrier, len(partners))

    def halo_send(t, img):
        base = K_HALO + 8 * t
        for i, d in enumerate(halo_dirs):
            if i < 2:
                send(img.at[15 if i == 0 else 0], hrow.at[t, i], base + i, near(*d))
            else:
                send(scol.at[t, 0 if i < 5 else 1], hcol.at[t, i - 2], base + i, near(*d))

    def halo_recv(t):
        base = K_HALO + 8 * t
        for i in range(8):
            got(base + i)
        above, below = row > 0, row < NROW - 1
        left, right = me > 0, me < NZ - 1

        def part(ok, v):
            return jnp.where(ok, v, jnp.zeros_like(v))

        xp[pl.ds(0, 32), :] = part(above, hrow[t, 0])
        xp[pl.ds(544, 32), :] = part(below, hrow[t, 1])
        for side, ok, dst in ((0, left, hl), (3, right, hr)):
            dst[0:1, :] = part(ok & above, hcol[t, side].astype(F32)[15:16, :])
            dst[1:17, :] = part(ok, hcol[t, side + 1].astype(F32))
            dst[17:18, :] = part(ok & below, hcol[t, side + 2].astype(F32)[0:1, :])

        lanes = lax.broadcasted_iota(jnp.int32, (32, CH), 0)

        def one(r, carry):
            at = pl.multiple_of(r * 32, 32)
            mid = xp[pl.ds(at, 32), :]
            c = mid.astype(F32)
            lf = jnp.where(lanes == 0, hl[pl.ds(r, 1), :], pltpu.roll(c, 1, 0))
            rt = jnp.where(lanes == 31, hr[pl.ds(r, 1), :], pltpu.roll(c, 31, 0))
            x3m[pl.ds(at, 32), 0:CH] = lf.astype(BF)
            x3m[pl.ds(at, 32), CH:2 * CH] = mid
            x3m[pl.ds(at, 32), 2 * CH:3 * CH] = rt.astype(BF)
            return carry

        return one

    def conv_map(w, j):
        total = mm(x3m[pl.ds(j * HALF, HALF), :], w[0])
        total += mm(x3m[pl.ds(j * HALF + 32, HALF), :], w[1])
        total += mm(x3m[pl.ds(j * HALF + 64, HALF), :], w[2])
        return total

    def turn(src, dst, taps):
        for a in taps:
            for b in range(3):
                dst[a, b * CH:(b + 1) * CH, :] = src[2 - a, (2 - b) * CH:(3 - b) * CH, :].T

    halo_send(0, in_ref)
    for d in range(1, NZ):
        send(tab.at[0], tab.at[d], K_TAB + d - 1, at_z(d))
    for buf in (xc3, xh3, d23, d13):
        for h in range(5):
            at = max(h * POS, 0)
            buf[at:at + 32, :] = jnp.zeros((32, 3 * CH), BF)
    acc[...] = jnp.zeros_like(acc)
    loads[1].wait()
    turn(w2_ref, w2t, (0, 1, 2))
    loads[0].wait()
    widen = halo_recv(0)

    def ag_key(right, s, j):
        return K_AG + (0 if right else 7) + (s * 2 + j if s < 3 else 6)

    def ag_send(right, s, j):
        src = feats.at[s if right else (NZ - s) % NZ, pl.ds(j * HALF, HALF), :]
        dst = feats.at[s + 1 if right else NZ - 1 - s, pl.ds(j * HALF, HALF), :]
        send(src, dst, ag_key(right, s, j), at_z(1 if right else -1))

    for j in range(2):
        lax.fori_loop(10 * j, 10 + 8 * j, widen, 0)
        pre = conv_map(tw_ref, j)
        feats[0, pl.ds(j * HALF, HALF), :] = (pre * jax.nn.sigmoid(pre)).astype(BF)
        ag_send(True, 0, j)
        ag_send(False, 0, j)
        slope_map[pl.ds(j * HALF, HALF), :] = silu_slope(pre)

    for d in range(1, NZ):
        got(K_TAB + d - 1)
    for h in range(4):
        base = jnp.zeros((1, 1), jnp.int32)
        for s in range(NZ):
            tile = lax.rem(me - s + NZ, NZ)
            word = tab[s, 0:1, :]
            hit = (word >> 7) == me * 4 + h
            value = (word & 127) + tile * PX
            base += jnp.sum(jnp.where(hit, value, 0), axis=1, keepdims=True)
        p = lax.broadcasted_iota(jnp.int32, (POS, 128), 0)
        i, j = p >> 4, p & 15
        ok = (i >= 1) & (i <= 14) & (j < 14)
        gcol[h] = jnp.where(ok, base + (i - 1) * 32 + j, -1)
        p = lax.broadcasted_iota(jnp.int32, (1, POS), 1)
        i, j = p >> 4, p & 15
        ok = (i >= 1) & (i <= 14) & (j < 14)
        grow[0:1, h * POS:(h + 1) * POS] = jnp.where(ok, base + (i - 1) * 32 + j, -1)

    def take(s, j):
        tile = lax.rem(me - s + NZ, NZ)
        first = tile * PX + j * HALF

        def one(h, carry):
            q = lax.broadcasted_iota(jnp.int32, (POS, 128), 1) + first
            g = gcol[h]
            hot = jnp.concatenate(
                [jnp.where(g == q, 1.0, 0.0), jnp.where(g == q + 128, 1.0, 0.0)], axis=1
            ).astype(BF)
            acc[h] += mm(hot, feats[s, pl.ds(j * HALF, HALF), :])
            return carry

        lax.fori_loop(0, 4, one, 0)

    take(0, 0)
    take(0, 1)

    loads[2].wait()
    loads[3].wait()

    def spread(i, carry):
        cotf[...] = cot_ref[i].astype(F32)
        for h in range(4):
            cots[h, i, 0:14, :] = cotf[:, h, :]
            cots[h, i, 14:16, :] = jnp.zeros((2, CH), F32)
        return carry

    lax.fori_loop(0, 14, spread, 0)
    for s in range(1, 4):
        for j in range(2):
            got(ag_key(True, s - 1, j))
            if s < 3 or j == 0:
                ag_send(True, s, j)
            got(ag_key(False, s - 1, j))
            if s < 3 or j == 1:
                ag_send(False, s, j)
            take(s, j)
            take(NZ - s, j)
            if s < 3:
                n = 2 * (s - 1) + j
                if n < 3:
                    turn(w1_ref, w1t, (n,))
                turn(tw_ref, twt, (n,) if n < 3 else ())
    got(ag_key(True, 3, 0))
    take(4, 0)
    got(ag_key(False, 3, 1))
    take(4, 1)

    inside = (lax.broadcasted_iota(jnp.int32, (224, CH), 0) & 15) < 14

    def put(buf, h, value):
        at = h * POS + 32
        mid = value.astype(BF)
        full = mid.astype(F32)
        buf[pl.ds(at, 224), 0:CH] = pltpu.roll(full, 1, 0).astype(BF)
        buf[pl.ds(at, 224), CH:2 * CH] = mid
        buf[pl.ds(at, 224), 2 * CH:3 * CH] = pltpu.roll(full, 223, 0).astype(BF)

    def conv_box(buf, w, h):
        at = h * POS + 16
        total = mm(buf[pl.ds(at, 224), :], w[0])
        total += mm(buf[pl.ds(at + 16, 224), :], w[1])
        total += mm(buf[pl.ds(at + 32, 224), :], w[2])
        return total

    def cut(v):
        return jnp.where(inside, v, 0.0)

    for h in range(4):
        put(xc3, h, acc[h, 16:240, :])
    for h in range(4):
        pre = conv_box(xc3, w1_ref, h)
        put(xh3, h, cut(pre * jax.nn.sigmoid(pre)))
        slope1[h] = silu_slope(pre)
    for h in range(4):
        pre = conv_box(xh3, w2_ref, h)
        put(d23, h, cut(cots[h].reshape(224, CH) * silu_slope(pre)))

    def term(d, j):
        tile = lax.rem(me + d + NZ, NZ)
        q = lax.broadcasted_iota(jnp.int32, (HALF, 4 * POS), 0) + (tile * PX + j * HALF)
        hot = jnp.where(q == grow[0:1, :], 1.0, 0.0).astype(BF)
        return mm(hot, bg[...])

    def rs_item(right, k):
        if k == 0:
            d, j = 4, 0
        else:
            d = 3 - (k - 1) // 2
            j = 1 if k % 2 == 1 else 0
        return d, (j if right else 1 - j)

    def rs_key(right, k):
        return K_RS + (0 if right else 7) + k

    def rs_step(k):
        for right in (True, False):
            d, j = rs_item(right, k)
            side = 0 if right else 1
            value = term(d if right else -d, j)
            if k >= 2:
                got(rs_key(right, k - 2))
                value += rs_r[side, k - 2].astype(F32)
            rs_s[side, k] = value.astype(BF)
            send(rs_s.at[side, k], rs_r.at[side, k], rs_key(right, k), at_z(1 if right else -1))

    def wgrad(g, buf, dbuf):
        for h in range(4):
            xt[:, h * POS:(h + 1) * POS] = buf[16 + h * POS:16 + (h + 1) * POS, CH:2 * CH].T

        for a in range(3):
            at = 32 - a * 16
            for b in range(3):
                value = mm(xt[...], dbuf[pl.ds(at, 4 * POS), (2 - b) * CH:(3 - b) * CH])
                low, high = value[:, 0:128], value[:, 128:256]
                own[g, a * 3 + b] = jnp.where(core == 0, low, high)
                snd[g, a * 3 + b] = jnp.where(core == 0, high, low).astype(BF)
            if a > 0:
                n = 2 * (1 - g) + a - 1
                span = pl.ds(PARTS[n][1], PARTS[n][2])
                send(snd.at[g, span], rc.at[g, span], K_AR + n * AR_N, sibling)

    def axes(n):
        if PARTS[n][3]:
            return at_x, px, NX, at_y, py, NY
        return at_y, py, NY, at_x, px, NX

    def ar1(n):
        g, t0, nt, _ = PARTS[n]
        k = K_AR + n * AR_N
        at1, p1, n1 = axes(n)[:3]
        got(k)

        def one(t, carry):
            v = own[g, t] + rc[g, t].astype(F32)
            own[g, t] = v
            s1[g, t] = v.astype(BF)
            return carry

        lax.fori_loop(t0, t0 + nt, one, 0)
        for d in range(1, 4):
            q = lax.rem(p1 + d, n1)
            src = s1.at[g, pl.ds(t0, nt), pl.ds(q * 64, 64), :]
            send(src, r1.at[n, d - 1, pl.ds(0, nt)], k + d, at1(d))

    def ar2(n):
        g, t0, nt, _ = PARTS[n]
        k = K_AR + n * AR_N
        at1, p1, n1, at2, p2, n2 = axes(n)
        for d in range(1, 4):
            got(k + d)

        def one(t, carry):
            v = own[g, t0 + t, pl.ds(p1 * 64, 64), :]
            for d in range(3):
                v += r1[n, d, t].astype(F32)
            t2[n, t] = v
            s2[n, t] = v.astype(BF)
            return carry

        lax.fori_loop(0, nt, one, 0)
        for d in range(1, 4):
            q = lax.rem(p2 + d, n2)
            src = s2.at[n, pl.ds(0, nt), pl.ds(q * 16, 16), :]
            send(src, r2.at[n, d - 1, pl.ds(0, nt)], k + 3 + d, at2(d))

    def owner(n, t):
        return t + (0 if PARTS[n][1] == 0 else 4)

    def z_copy(src, dst, ks, kr, to):
        return pltpu.make_async_remote_copy(
            src_ref=src, dst_ref=dst, send_sem=ssem.at[ks], recv_sem=rsem.at[kr],
            device_id=(row, to), device_id_type=MESH,
        )

    def ar3(n):
        nt = PARTS[n][2]
        k = K_AR + n * AR_N
        p2 = axes(n)[4]
        for d in range(1, 4):
            got(k + 3 + d)
        v = t2[n, 0:nt, pl.ds(p2 * 16, 16), :]
        for d in range(3):
            v += r2[n, d, 0:nt].astype(F32)
        t3[n, 0:nt] = v
        s3[n, 0:nt] = v.astype(BF)
        for t in range(nt):
            to = owner(n, t)

            @pl.when(me != to)
            def _():
                z_copy(s3.at[n, t], r3.at[n, me], k + 7 + t, k + 7 + me, to).start()

    def ar4(n):
        nt = PARTS[n][2]
        k = K_AR + n * AR_N
        first = owner(n, 0)

        @pl.when((me >= first) & (me < first + nt))
        def _():
            for p in range(NZ):
                @pl.when(me != p)
                def _():
                    z_copy(s3.at[n, 0], r3.at[n, p], k + 7, k + 7 + p, p).wait_recv()
            v = t3[n, me - first]
            for p in range(NZ):
                v += jnp.where(me != p, r3[n, p].astype(F32), 0.0)
            zb[n, me - first] = v.astype(BF)
            part = zb.at[n, me - first]
            for p in range(NZ):
                @pl.when(me != p)
                def _():
                    z_copy(part, part, k + 15 + p, k + 15 + me - first, p).start()

    def ar5(n):
        g, t0, nt, _ = PARTS[n]
        k = K_AR + n * AR_N
        at1, p1, n1, at2, p2, n2 = axes(n)
        first = owner(n, 0)
        for t in range(nt):
            @pl.when(me != owner(n, t))
            def _():
                z_copy(zb.at[n, t], zb.at[n, t], k + 15, k + 15 + t, owner(n, t)).wait_recv()
        at = pl.multiple_of(p1 * 64 + p2 * 16, 16)
        gsum_ref[g, core, t0:t0 + nt, pl.ds(at, 16), :] = zb[n, 0:nt]
        part = gsum_ref.at[g, core, pl.ds(t0, nt), pl.ds(at, 16), :]
        for d in range(1, 4):
            send(part, part, k + 22 + d, at2(d))

    def z_sent(n):
        nt = PARTS[n][2]
        k = K_AR + n * AR_N
        first = owner(n, 0)
        for t in range(nt):
            @pl.when(me != owner(n, t))
            def _():
                z_copy(s3.at[n, t], r3.at[n, me], k + 7 + t, k + 7, owner(n, t)).wait_send()

        @pl.when((me >= first) & (me < first + nt))
        def _():
            for p in range(NZ):
                @pl.when(me != p)
                def _():
                    z_copy(zb.at[n, 0], zb.at[n, 0], k + 15 + p, k + 15, p).wait_send()

    def ar6(n):
        g, t0, nt, _ = PARTS[n]
        k = K_AR + n * AR_N
        at1, p1, n1 = axes(n)[:3]
        for d in range(1, 4):
            got(k + 22 + d)
        part = gsum_ref.at[g, core, pl.ds(t0, nt), pl.ds(p1 * 64, 64), :]
        for d in range(1, 4):
            send(part, part, k + 25 + d, at1(d))
        send(part, part, k + 29, sibling)

    def ar7(n):
        g, t0, nt, _ = PARTS[n]
        k = K_AR + n * AR_N
        at1, p1, n1 = axes(n)[:3]
        for d in (1, 3, 2):
            got(k + 25 + d)
            q = lax.rem(p1 - d + n1, n1)
            part = gsum_ref.at[g, core, pl.ds(t0, nt), pl.ds(q * 64, 64), :]
            send(part, part, k + 29 + d, sibling)

    def both(stage, g):
        stage(2 * (1 - g))
        stage(2 * (1 - g) + 1)

    wgrad(1, xh3, d23)
    for h in range(4):
        put(d13, h, cut(conv_box(d23, w2t, h) * slope1[h]))
    wgrad(0, xc3, d13)
    both(ar1, 1)
    for h in range(4):
        bg[h * POS:h * POS + 16, :] = jnp.zeros((16, CH), BF)
        bg[h * POS + 240:(h + 1) * POS, :] = jnp.zeros((16, CH), BF)
        bg[h * POS + 16:h * POS + 240, :] = conv_box(d13, w1t, h).astype(BF)
    rs_step(0)
    rs_step(1)
    both(ar1, 0)
    both(ar2, 1)
    rs_step(2)
    both(ar3, 1)
    both(ar2, 0)
    rs_step(3)
    both(ar3, 0)
    rs_step(4)
    both(ar4, 1)
    rs_step(5)
    both(ar4, 0)
    both(ar5, 1)
    rs_step(6)
    both(ar5, 0)
    both(ar6, 1)
    both(ar6, 0)
    both(ar7, 1)

    for j in range(2):
        total = term(0, j)
        for right in (True, False):
            k = 6 if rs_item(right, 6)[1] == j else 5
            got(rs_key(right, k))
            total += rs_r[0 if right else 1, k].astype(F32)
        grad = (total * slope_map[pl.ds(j * HALF, HALF), :]).astype(BF)
        xp[pl.ds(32 + j * HALF, HALF), :] = grad
        dm[8 * j:8 * j + 8] = grad.reshape(8, 32, CH)
        xf[8 * j:8 * j + 8] = grad.astype(F32).reshape(8, 32, CH)
    scol[1, 0] = xf[:, 31, :].astype(BF)
    scol[1, 1] = xf[:, 0, :].astype(BF)
    halo_send(1, dm)
    both(ar7, 0)
    lax.fori_loop(0, 18, halo_recv(1), 0)
    for j in range(2):
        gmap_ref[8 * j:8 * j + 8] = conv_map(twt, j).astype(BF).reshape(8, 32, CH)
    for n in range(4):
        for d in range(4):
            got(K_AR + n * AR_N + 29 + d)
        z_sent(n)
    for k in sorted(live):
        live[k].wait_send()


def finish(map_ref, sums_ref, out_ref, first_ref, second_ref):
    factor = 1.0 / math.sqrt(32 * 8 * 4 * 14 * 14)
    out_ref[...] = map_ref[...]
    for g, ref in enumerate((first_ref, second_ref)):
        for half in range(2):
            ref[:, :, half * 128:half * 128 + 128] = sums_ref[g, half].astype(F32) * factor


def step(in_map, tile_w, head_w1, head_w2, box_row, box_col, box_target, head_cot):
    vm = pltpu.VMEM
    scratch = [
        vm((3, 3 * CH, CH), BF),
        vm((3, 3 * CH, CH), BF),
        vm((3, 3 * CH, CH), BF),
        vm((14, 14, 4, CH), BF),
        vm((16, 32, CH), F32),
        vm((576, CH), BF),
        vm((576, 3 * CH), BF),
        vm((PX, CH), F32),
        vm((2, 2, 16, CH), BF),
        vm((2, 2, 32, CH), BF),
        vm((2, 6, 16, CH), BF),
        vm((24, CH), F32),
        vm((24, CH), F32),
        vm((NZ, 8, 128), jnp.int32),
        vm((4, POS, 128), jnp.int32),
        vm((1, 4 * POS), jnp.int32),
        vm((NZ, PX, CH), BF),
        vm((4, POS, CH), F32),
        vm((1056, 3 * CH), BF),
        vm((1056, 3 * CH), BF),
        vm((1056, 3 * CH), BF),
        vm((1056, 3 * CH), BF),
        vm((4, 224, CH), F32),
        vm((14, 4, CH), F32),
        vm((4, 14, 16, CH), F32),
        vm((CH, 4 * POS), BF),
        vm((3, 3 * CH, CH), BF),
        vm((3, 3 * CH, CH), BF),
        vm((3, 3 * CH, CH), BF),
        vm((4 * POS, CH), BF),
        vm((2, 7, HALF, CH), BF),
        vm((2, 7, HALF, CH), BF),
        vm((16, 32, CH), BF),
        vm((2, 9, 256, 128), F32),
        vm((2, 9, 256, 128), BF),
        vm((2, 9, 256, 128), BF),
        vm((2, 9, 256, 128), BF),
        vm((4, 3, 5, 64, 128), BF),
        vm((4, 5, 64, 128), F32),
        vm((4, 5, 64, 128), BF),
        vm((4, 3, 5, 16, 128), BF),
        vm((4, 5, 16, 128), F32),
        vm((4, 5, 16, 128), BF),
        vm((4, NZ, 16, 128), BF),
        vm((4, 5, 16, 128), BF),
        pltpu.SemaphoreType.DMA((N_SEM,)),
        pltpu.SemaphoreType.DMA((N_SEM,)),
        pltpu.SemaphoreType.DMA((4,)),
    ]
    in_vmem = pl.BlockSpec(memory_space=pltpu.VMEM)
    in_any = pl.BlockSpec(memory_space=pl.ANY)
    grad_map, sums = pl.pallas_call(
        kernel,
        out_shape=(
            jax.ShapeDtypeStruct((16, 32, CH), BF),
            jax.ShapeDtypeStruct((2, 2, 9, 256, 128), BF),
        ),
        in_specs=[in_vmem] + [in_any] * 3 + [in_vmem] * 3 + [in_any],
        out_specs=(in_vmem, in_vmem),
        scratch_shapes=scratch,
        compiler_params=pltpu.CompilerParams(
            collective_id=0, has_side_effects=True, vmem_limit_bytes=58 * 1024 * 1024
        ),
        cost_estimate=pl.CostEstimate(flops=8 * 10**9, bytes_accessed=10**7, transcendentals=10**6),
    )(
        in_map,
        tile_w.reshape(3, 3 * CH, CH),
        head_w1.reshape(3, 3 * CH, CH),
        head_w2.reshape(3, 3 * CH, CH),
        box_row.T,
        box_col.T,
        box_target.T,
        head_cot[:, 0].transpose(1, 2, 0, 3),
    )
    grad_map, first, second = pl.pallas_call(
        finish,
        grid=(1,),
        out_shape=(
            jax.ShapeDtypeStruct((16, 32, CH), BF),
            jax.ShapeDtypeStruct((9, CH, CH), F32),
            jax.ShapeDtypeStruct((9, CH, CH), F32),
        ),
        in_specs=[
            pl.BlockSpec((16, 32, CH), lambda i: (0, 0, 0)),
            pl.BlockSpec((2, 2, 9, CH, 128), lambda i: (0, 0, i, 0, 0)),
        ],
        out_specs=(
            pl.BlockSpec((16, 32, CH), lambda i: (0, 0, 0)),
            pl.BlockSpec((9, CH, CH), lambda i: (i, 0, 0)),
            pl.BlockSpec((9, CH, CH), lambda i: (i, 0, 0)),
        ),
    )(grad_map, sums)
    return grad_map, first.reshape(3, 3, CH, CH), second.reshape(3, 3, CH, CH)


def solution(mesh):
    in_specs = (
        P("row", "col", None),
        P(),
        P(),
        P(),
        P("row", "col"),
        P("row", "col"),
        P("row", "col"),
        P("row", "col", None, None, None),
    )
    out_specs = (P("row", "col", None), P(), P())
    return jax.shard_map(step, mesh=mesh, in_specs=in_specs, out_specs=out_specs, check_vma=False)
```

```python
import math

import jax
import jax.numpy as jnp
from jax import lax
from jax.experimental import pallas as pl
from jax.experimental.pallas import tpu as pltpu
from jax.sharding import PartitionSpec as P

MESH = pl.DeviceIdType.MESH
BF = jnp.bfloat16
F32 = jnp.float32
NZ = 8
NX = 4
NY = 4
NROW = 32
PX = 512
HALF = 256
POS = 256
CH = 256
K_HALO = 0
K_TAB = 16
K_AG = 23
K_RS = 37
K_AR = 51
AR_N = 33
N_SEM = K_AR + 4 * AR_N
PARTS = ((1, 0, 5, False), (1, 5, 4, True), (0, 0, 5, True), (0, 5, 4, False))


def silu_slope(values):
    sigma = jax.nn.sigmoid(values)
    return sigma * (1.0 + values * (1.0 - sigma))


def mm(a, b):
    return jnp.dot(a, b, preferred_element_type=F32)


def kernel(
    in_ref, tw_any, w1_any, w2_any, brow_ref, bcol_ref, btgt_ref, cot_any,
    gmap_ref, gsum_ref,
    tw_ref, w1_ref, w2_ref, cot_ref, xf, xp, x3m, slope_map, scol, hrow, hcol, hl, hr,
    tab, gcol, grow, feats, acc, xc3, xh3, d23, d13, slope1, cotf, cots, xt,
    twt, w1t, w2t, bg, rs_s, rs_r, dm,
    own, snd, rc, s1, r1, t2, s2, r2, t3, s3, r3, zb,
    ssem, rsem, lsem,
):
    row = lax.axis_index("row")
    me = lax.axis_index("col")
    px = row // 8
    py = lax.rem(row // 2, NY)
    core = lax.rem(row, 2)

    def at_x(d):
        return (lax.rem(px + d, NX) * 8 + py * 2 + core, me)

    def at_y(d):
        return (px * 8 + lax.rem(py + d, NY) * 2 + core, me)

    def at_z(d):
        return (row, lax.rem(me + d + NZ, NZ))

    sibling = (row + 1 - 2 * core, me)

    def near(dr, dc):
        return (lax.rem(row + dr + NROW, NROW), lax.rem(me + dc + NZ, NZ))

    live = {}

    def send(src, dst, k, dev):
        copy = pltpu.make_async_remote_copy(
            src_ref=src, dst_ref=dst, send_sem=ssem.at[k], recv_sem=rsem.at[k],
            device_id=dev, device_id_type=MESH,
        )
        copy.start()
        live[k] = copy

    def got(k):
        live[k].wait_recv()

    halo_dirs = [(1, 0), (-1, 0), (1, 1), (0, 1), (-1, 1), (1, -1), (0, -1), (-1, -1)]

    barrier = pltpu.get_barrier_semaphore()
    partners = [near(*d) for d in halo_dirs]
    partners += [at_z(d) for d in range(2, 7)]
    partners += [at_x(d) for d in range(1, 4)] + [at_y(d) for d in range(1, 4)] + [sibling]
    for dev in partners:
        pl.semaphore_signal(barrier, inc=1, device_id=dev, device_id_type=MESH)

    loads = []
    for n, (src, dst) in enumerate(
        ((tw_any, tw_ref), (w2_any, w2_ref), (w1_any, w1_ref), (cot_any, cot_ref))
    ):
        loads.append(pltpu.make_async_copy(src, dst, lsem.at[n]))
        loads[n].start()

    xf[...] = in_ref[...].astype(F32)
    scol[0, 0] = xf[:, 31, :].astype(BF)
    scol[0, 1] = xf[:, 0, :].astype(BF)
    tab[0] = jnp.full((8, 128), -128, jnp.int32)
    tab[0, 0:1, 0:16] = btgt_ref[...] * 128 + brow_ref[...] * 32 + bcol_ref[...]
    xp[pl.ds(32, PX), :] = in_ref[...].reshape(PX, CH)

    pl.semaphore_wait(barrier, len(partners))

    def halo_send(t, img):
        base = K_HALO + 8 * t
        for i, d in enumerate(halo_dirs):
            if i < 2:
                send(img.at[15 if i == 0 else 0], hrow.at[t, i], base + i, near(*d))
            else:
                send(scol.at[t, 0 if i < 5 else 1], hcol.at[t, i - 2], base + i, near(*d))

    def halo_recv(t):
        base = K_HALO + 8 * t
        for i in range(8):
            got(base + i)
        above, below = row > 0, row < NROW - 1
        left, right = me > 0, me < NZ - 1

        def part(ok, v):
            return jnp.where(ok, v, jnp.zeros_like(v))

        xp[pl.ds(0, 32), :] = part(above, hrow[t, 0])
        xp[pl.ds(544, 32), :] = part(below, hrow[t, 1])
        for side, ok, dst in ((0, left, hl), (3, right, hr)):
            dst[0:1, :] = part(ok & above, hcol[t, side].astype(F32)[15:16, :])
            dst[1:17, :] = part(ok, hcol[t, side + 1].astype(F32))
            dst[17:18, :] = part(ok & below, hcol[t, side + 2].astype(F32)[0:1, :])

        lanes = lax.broadcasted_iota(jnp.int32, (32, CH), 0)

        def one(r, carry):
            at = pl.multiple_of(r * 32, 32)
            mid = xp[pl.ds(at, 32), :]
            c = mid.astype(F32)
            lf = jnp.where(lanes == 0, hl[pl.ds(r, 1), :], pltpu.roll(c, 1, 0))
            rt = jnp.where(lanes == 31, hr[pl.ds(r, 1), :], pltpu.roll(c, 31, 0))
            x3m[pl.ds(at, 32), 0:CH] = lf.astype(BF)
            x3m[pl.ds(at, 32), CH:2 * CH] = mid
            x3m[pl.ds(at, 32), 2 * CH:3 * CH] = rt.astype(BF)
            return carry

        return one

    def conv_map(w, j):
        total = mm(x3m[pl.ds(j * HALF, HALF), :], w[0])
        total += mm(x3m[pl.ds(j * HALF + 32, HALF), :], w[1])
        total += mm(x3m[pl.ds(j * HALF + 64, HALF), :], w[2])
        return total

    def turn(src, dst, taps):
        for a in taps:
            for b in range(3):
                dst[a, b * CH:(b + 1) * CH, :] = src[2 - a, (2 - b) * CH:(3 - b) * CH, :].T

    halo_send(0, in_ref)
    for d in range(1, NZ):
        send(tab.at[0], tab.at[d], K_TAB + d - 1, at_z(d))
    for buf in (xc3, xh3, d23, d13):
        for h in range(5):
            at = max(h * POS, 0)
            buf[at:at + 32, :] = jnp.zeros((32, 3 * CH), BF)
    acc[...] = jnp.zeros_like(acc)
    loads[1].wait()
    turn(w2_ref, w2t, (0, 1, 2))
    loads[0].wait()
    widen = halo_recv(0)

    def ag_key(right, s, j):
        return K_AG + (0 if right else 7) + (s * 2 + j if s < 3 else 6)

    def ag_send(right, s, j):
        src = feats.at[s if right else (NZ - s) % NZ, pl.ds(j * HALF, HALF), :]
        dst = feats.at[s + 1 if right else NZ - 1 - s, pl.ds(j * HALF, HALF), :]
        send(src, dst, ag_key(right, s, j), at_z(1 if right else -1))

    for j in range(2):
        lax.fori_loop(10 * j, 10 + 8 * j, widen, 0)
        pre = conv_map(tw_ref, j)
        feats[0, pl.ds(j * HALF, HALF), :] = (pre * jax.nn.sigmoid(pre)).astype(BF)
        ag_send(True, 0, j)
        ag_send(False, 0, j)
        slope_map[pl.ds(j * HALF, HALF), :] = silu_slope(pre)

    for d in range(1, NZ):
        got(K_TAB + d - 1)
    for h in range(4):
        base = jnp.zeros((1, 1), jnp.int32)
        for s in range(NZ):
            tile = lax.rem(me - s + NZ, NZ)
            word = tab[s, 0:1, :]
            hit = (word >> 7) == me * 4 + h
            value = (word & 127) + tile * PX
            base += jnp.sum(jnp.where(hit, value, 0), axis=1, keepdims=True)
        p = lax.broadcasted_iota(jnp.int32, (POS, 128), 0)
        i, j = p >> 4, p & 15
        ok = (i >= 1) & (i <= 14) & (j < 14)
        gcol[h] = jnp.where(ok, base + (i - 1) * 32 + j, -1)
        p = lax.broadcasted_iota(jnp.int32, (1, POS), 1)
        i, j = p >> 4, p & 15
        ok = (i >= 1) & (i <= 14) & (j < 14)
        grow[0:1, h * POS:(h + 1) * POS] = jnp.where(ok, base + (i - 1) * 32 + j, -1)

    def take(s, j):
        tile = lax.rem(me - s + NZ, NZ)
        first = tile * PX + j * HALF

        def one(h, carry):
            q = lax.broadcasted_iota(jnp.int32, (POS, 128), 1) + first
            g = gcol[h]
            hot = jnp.concatenate(
                [jnp.where(g == q, 1.0, 0.0), jnp.where(g == q + 128, 1.0, 0.0)], axis=1
            ).astype(BF)
            acc[h] += mm(hot, feats[s, pl.ds(j * HALF, HALF), :])
            return carry

        lax.fori_loop(0, 4, one, 0)

    take(0, 0)
    take(0, 1)

    loads[2].wait()
    loads[3].wait()

    def spread(i, carry):
        cotf[...] = cot_ref[i].astype(F32)
        for h in range(4):
            cots[h, i, 0:14, :] = cotf[:, h, :]
            cots[h, i, 14:16, :] = jnp.zeros((2, CH), F32)
        return carry

    lax.fori_loop(0, 14, spread, 0)
    for s in range(1, 4):
        for j in range(2):
            got(ag_key(True, s - 1, j))
            if s < 3 or j == 0:
                ag_send(True, s, j)
            got(ag_key(False, s - 1, j))
            if s < 3 or j == 1:
                ag_send(False, s, j)
            take(s, j)
            take(NZ - s, j)
            if s < 3:
                n = 2 * (s - 1) + j
                if n < 3:
                    turn(w1_ref, w1t, (n,))
                turn(tw_ref, twt, (n,) if n < 3 else ())
    got(ag_key(True, 3, 0))
    take(4, 0)
    got(ag_key(False, 3, 1))
    take(4, 1)

    inside = (lax.broadcasted_iota(jnp.int32, (224, CH), 0) & 15) < 14

    def put(buf, h, value):
        at = h * POS + 32
        mid = value.astype(BF)
        full = mid.astype(F32)
        buf[pl.ds(at, 224), 0:CH] = pltpu.roll(full, 1, 0).astype(BF)
        buf[pl.ds(at, 224), CH:2 * CH] = mid
        buf[pl.ds(at, 224), 2 * CH:3 * CH] = pltpu.roll(full, 223, 0).astype(BF)

    def conv_box(buf, w, h):
        at = h * POS + 16
        total = mm(buf[pl.ds(at, 224), :], w[0])
        total += mm(buf[pl.ds(at + 16, 224), :], w[1])
        total += mm(buf[pl.ds(at + 32, 224), :], w[2])
        return total

    def cut(v):
        return jnp.where(inside, v, 0.0)

    for h in range(4):
        put(xc3, h, acc[h, 16:240, :])
    for h in range(4):
        pre = conv_box(xc3, w1_ref, h)
        put(xh3, h, cut(pre * jax.nn.sigmoid(pre)))
        slope1[h] = silu_slope(pre)
    for h in range(4):
        pre = conv_box(xh3, w2_ref, h)
        put(d23, h, cut(cots[h].reshape(224, CH) * silu_slope(pre)))

    def term(d, j):
        tile = lax.rem(me + d + NZ, NZ)
        q = lax.broadcasted_iota(jnp.int32, (HALF, 4 * POS), 0) + (tile * PX + j * HALF)
        hot = jnp.where(q == grow[0:1, :], 1.0, 0.0).astype(BF)
        return mm(hot, bg[...])

    def rs_item(right, k):
        if k == 0:
            d, j = 4, 0
        else:
            d = 3 - (k - 1) // 2
            j = 1 if k % 2 == 1 else 0
        return d, (j if right else 1 - j)

    def rs_key(right, k):
        return K_RS + (0 if right else 7) + k

    def rs_step(k):
        for right in (True, False):
            d, j = rs_item(right, k)
            side = 0 if right else 1
            value = term(d if right else -d, j)
            if k >= 2:
                got(rs_key(right, k - 2))
                value += rs_r[side, k - 2].astype(F32)
            rs_s[side, k] = value.astype(BF)
            send(rs_s.at[side, k], rs_r.at[side, k], rs_key(right, k), at_z(1 if right else -1))

    def wgrad(g, buf, dbuf):
        for h in range(4):
            xt[:, h * POS:(h + 1) * POS] = buf[16 + h * POS:16 + (h + 1) * POS, CH:2 * CH].T

        for a in range(3):
            at = 32 - a * 16
            for b in range(3):
                value = mm(xt[...], dbuf[pl.ds(at, 4 * POS), (2 - b) * CH:(3 - b) * CH])
                low, high = value[:, 0:128], value[:, 128:256]
                own[g, a * 3 + b] = jnp.where(core == 0, low, high)
                snd[g, a * 3 + b] = jnp.where(core == 0, high, low).astype(BF)
            if a > 0:
                n = 2 * (1 - g) + a - 1
                span = pl.ds(PARTS[n][1], PARTS[n][2])
                send(snd.at[g, span], rc.at[g, span], K_AR + n * AR_N, sibling)

    def axes(n):
        if PARTS[n][3]:
            return at_x, px, NX, at_y, py, NY
        return at_y, py, NY, at_x, px, NX

    def ar1(n):
        g, t0, nt, _ = PARTS[n]
        k = K_AR + n * AR_N
        at1, p1, n1 = axes(n)[:3]
        got(k)

        def one(t, carry):
            v = own[g, t] + rc[g, t].astype(F32)
            own[g, t] = v
            s1[g, t] = v.astype(BF)
            return carry

        lax.fori_loop(t0, t0 + nt, one, 0)
        for d in range(1, 4):
            q = lax.rem(p1 + d, n1)
            src = s1.at[g, pl.ds(t0, nt), pl.ds(q * 64, 64), :]
            send(src, r1.at[n, d - 1, pl.ds(0, nt)], k + d, at1(d))

    def ar2(n):
        g, t0, nt, _ = PARTS[n]
        k = K_AR + n * AR_N
        at1, p1, n1, at2, p2, n2 = axes(n)
        for d in range(1, 4):
            got(k + d)

        def one(t, carry):
            v = own[g, t0 + t, pl.ds(p1 * 64, 64), :]
            for d in range(3):
                v += r1[n, d, t].astype(F32)
            t2[n, t] = v
            s2[n, t] = v.astype(BF)
            return carry

        lax.fori_loop(0, nt, one, 0)
        for d in range(1, 4):
            q = lax.rem(p2 + d, n2)
            src = s2.at[n, pl.ds(0, nt), pl.ds(q * 16, 16), :]
            send(src, r2.at[n, d - 1, pl.ds(0, nt)], k + 3 + d, at2(d))

    def owner(n, t):
        return t + (0 if PARTS[n][1] == 0 else 4)

    def z_copy(src, dst, ks, kr, to):
        return pltpu.make_async_remote_copy(
            src_ref=src, dst_ref=dst, send_sem=ssem.at[ks], recv_sem=rsem.at[kr],
            device_id=(row, to), device_id_type=MESH,
        )

    def ar3(n):
        nt = PARTS[n][2]
        k = K_AR + n * AR_N
        p2 = axes(n)[4]
        for d in range(1, 4):
            got(k + 3 + d)
        v = t2[n, 0:nt, pl.ds(p2 * 16, 16), :]
        for d in range(3):
            v += r2[n, d, 0:nt].astype(F32)
        t3[n, 0:nt] = v
        s3[n, 0:nt] = v.astype(BF)
        for t in range(nt):
            to = owner(n, t)

            @pl.when(me != to)
            def _():
                z_copy(s3.at[n, t], r3.at[n, me], k + 7 + t, k + 7 + me, to).start()

    def ar4(n):
        nt = PARTS[n][2]
        k = K_AR + n * AR_N
        first = owner(n, 0)

        @pl.when((me >= first) & (me < first + nt))
        def _():
            for p in range(NZ):
                @pl.when(me != p)
                def _():
                    z_copy(s3.at[n, 0], r3.at[n, p], k + 7, k + 7 + p, p).wait_recv()
            v = t3[n, me - first]
            for p in range(NZ):
                v += jnp.where(me != p, r3[n, p].astype(F32), 0.0)
            zb[n, me - first] = v.astype(BF)
            part = zb.at[n, me - first]
            for p in range(NZ):
                @pl.when(me != p)
                def _():
                    z_copy(part, part, k + 15 + p, k + 15 + me - first, p).start()

    def ar5(n):
        g, t0, nt, _ = PARTS[n]
        k = K_AR + n * AR_N
        at1, p1, n1, at2, p2, n2 = axes(n)
        first = owner(n, 0)
        for t in range(nt):
            @pl.when(me != owner(n, t))
            def _():
                z_copy(zb.at[n, t], zb.at[n, t], k + 15, k + 15 + t, owner(n, t)).wait_recv()
        at = pl.multiple_of(p1 * 64 + p2 * 16, 16)
        gsum_ref[g, core, t0:t0 + nt, pl.ds(at, 16), :] = zb[n, 0:nt]
        part = gsum_ref.at[g, core, pl.ds(t0, nt), pl.ds(at, 16), :]
        for d in range(1, 4):
            send(part, part, k + 22 + d, at2(d))

    def z_sent(n):
        nt = PARTS[n][2]
        k = K_AR + n * AR_N
        first = owner(n, 0)
        for t in range(nt):
            @pl.when(me != owner(n, t))
            def _():
                z_copy(s3.at[n, t], r3.at[n, me], k + 7 + t, k + 7, owner(n, t)).wait_send()

        @pl.when((me >= first) & (me < first + nt))
        def _():
            for p in range(NZ):
                @pl.when(me != p)
                def _():
                    z_copy(zb.at[n, 0], zb.at[n, 0], k + 15 + p, k + 15, p).wait_send()

    def ar6(n):
        g, t0, nt, _ = PARTS[n]
        k = K_AR + n * AR_N
        at1, p1, n1 = axes(n)[:3]
        for d in range(1, 4):
            got(k + 22 + d)
        part = gsum_ref.at[g, core, pl.ds(t0, nt), pl.ds(p1 * 64, 64), :]
        for d in range(1, 4):
            send(part, part, k + 25 + d, at1(d))
        send(part, part, k + 29, sibling)

    def ar7(n):
        g, t0, nt, _ = PARTS[n]
        k = K_AR + n * AR_N
        at1, p1, n1 = axes(n)[:3]
        for d in (1, 3, 2):
            got(k + 25 + d)
            q = lax.rem(p1 - d + n1, n1)
            part = gsum_ref.at[g, core, pl.ds(t0, nt), pl.ds(q * 64, 64), :]
            send(part, part, k + 29 + d, sibling)

    def both(stage, g):
        stage(2 * (1 - g))
        stage(2 * (1 - g) + 1)

    wgrad(1, xh3, d23)
    for h in range(4):
        put(d13, h, cut(conv_box(d23, w2t, h) * slope1[h]))
    wgrad(0, xc3, d13)
    both(ar1, 1)
    for h in range(4):
        bg[h * POS:h * POS + 16, :] = jnp.zeros((16, CH), BF)
        bg[h * POS + 240:(h + 1) * POS, :] = jnp.zeros((16, CH), BF)
        bg[h * POS + 16:h * POS + 240, :] = conv_box(d13, w1t, h).astype(BF)
    rs_step(0)
    both(ar1, 0)
    rs_step(1)
    both(ar2, 1)
    rs_step(2)
    both(ar2, 0)
    both(ar3, 1)
    both(ar3, 0)
    rs_step(3)
    both(ar4, 1)
    rs_step(4)
    both(ar4, 0)
    both(ar5, 1)
    rs_step(5)
    both(ar5, 0)
    both(ar6, 1)
    rs_step(6)
    both(ar6, 0)
    both(ar7, 1)

    for j in range(2):
        total = term(0, j)
        for right in (True, False):
            k = 6 if rs_item(right, 6)[1] == j else 5
            got(rs_key(right, k))
            total += rs_r[0 if right else 1, k].astype(F32)
        grad = (total * slope_map[pl.ds(j * HALF, HALF), :]).astype(BF)
        xp[pl.ds(32 + j * HALF, HALF), :] = grad
        dm[8 * j:8 * j + 8] = grad.reshape(8, 32, CH)
        xf[8 * j:8 * j + 8] = grad.astype(F32).reshape(8, 32, CH)
    scol[1, 0] = xf[:, 31, :].astype(BF)
    scol[1, 1] = xf[:, 0, :].astype(BF)
    halo_send(1, dm)
    both(ar7, 0)
    lax.fori_loop(0, 18, halo_recv(1), 0)
    for j in range(2):
        gmap_ref[8 * j:8 * j + 8] = conv_map(twt, j).astype(BF).reshape(8, 32, CH)
    for n in range(4):
        for d in range(4):
            got(K_AR + n * AR_N + 29 + d)
        z_sent(n)
    for k in sorted(live):
        live[k].wait_send()


def finish(map_ref, sums_ref, out_ref, first_ref, second_ref, held, made, isem, osem, msem):
    factor = 1.0 / math.sqrt(32 * 8 * 4 * 14 * 14)
    whole = pltpu.make_async_copy(map_ref, out_ref, msem)
    whole.start()
    loads, stores = [], []
    for t in range(3):
        span = pl.ds(3 * t, 3)
        loads.append(pltpu.make_async_copy(sums_ref.at[:, :, span], held.at[:, :, span], isem.at[t]))
        loads[t].start()
    for t in range(3):
        loads[t].wait()
        for g, ref in enumerate((first_ref, second_ref)):
            for half in range(2):
                low = half * 128
                made[g, 3 * t:3 * t + 3, :, low:low + 128] = (
                    held[g, half, 3 * t:3 * t + 3].astype(F32) * factor
                )
            span = pl.ds(3 * t, 3)
            store = pltpu.make_async_copy(made.at[g, span], ref.at[span], osem.at[2 * t + g])
            store.start()
            stores.append(store)
    for store in stores:
        store.wait()
    whole.wait()


def step(in_map, tile_w, head_w1, head_w2, box_row, box_col, box_target, head_cot):
    vm = pltpu.VMEM
    scratch = [
        vm((3, 3 * CH, CH), BF),
        vm((3, 3 * CH, CH), BF),
        vm((3, 3 * CH, CH), BF),
        vm((14, 14, 4, CH), BF),
        vm((16, 32, CH), F32),
        vm((576, CH), BF),
        vm((576, 3 * CH), BF),
        vm((PX, CH), F32),
        vm((2, 2, 16, CH), BF),
        vm((2, 2, 32, CH), BF),
        vm((2, 6, 16, CH), BF),
        vm((24, CH), F32),
        vm((24, CH), F32),
        vm((NZ, 8, 128), jnp.int32),
        vm((4, POS, 128), jnp.int32),
        vm((1, 4 * POS), jnp.int32),
        vm((NZ, PX, CH), BF),
        vm((4, POS, CH), F32),
        vm((1056, 3 * CH), BF),
        vm((1056, 3 * CH), BF),
        vm((1056, 3 * CH), BF),
        vm((1056, 3 * CH), BF),
        vm((4, 224, CH), F32),
        vm((14, 4, CH), F32),
        vm((4, 14, 16, CH), F32),
        vm((CH, 4 * POS), BF),
        vm((3, 3 * CH, CH), BF),
        vm((3, 3 * CH, CH), BF),
        vm((3, 3 * CH, CH), BF),
        vm((4 * POS, CH), BF),
        vm((2, 7, HALF, CH), BF),
        vm((2, 7, HALF, CH), BF),
        vm((16, 32, CH), BF),
        vm((2, 9, 256, 128), F32),
        vm((2, 9, 256, 128), BF),
        vm((2, 9, 256, 128), BF),
        vm((2, 9, 256, 128), BF),
        vm((4, 3, 5, 64, 128), BF),
        vm((4, 5, 64, 128), F32),
        vm((4, 5, 64, 128), BF),
        vm((4, 3, 5, 16, 128), BF),
        vm((4, 5, 16, 128), F32),
        vm((4, 5, 16, 128), BF),
        vm((4, NZ, 16, 128), BF),
        vm((4, 5, 16, 128), BF),
        pltpu.SemaphoreType.DMA((N_SEM,)),
        pltpu.SemaphoreType.DMA((N_SEM,)),
        pltpu.SemaphoreType.DMA((4,)),
    ]
    in_vmem = pl.BlockSpec(memory_space=pltpu.VMEM)
    in_any = pl.BlockSpec(memory_space=pl.ANY)
    grad_map, sums = pl.pallas_call(
        kernel,
        out_shape=(
            jax.ShapeDtypeStruct((16, 32, CH), BF),
            jax.ShapeDtypeStruct((2, 2, 9, 256, 128), BF),
        ),
        in_specs=[in_vmem] + [in_any] * 3 + [in_vmem] * 3 + [in_any],
        out_specs=(in_vmem, in_vmem),
        scratch_shapes=scratch,
        compiler_params=pltpu.CompilerParams(
            collective_id=0, has_side_effects=True, vmem_limit_bytes=58 * 1024 * 1024
        ),
        cost_estimate=pl.CostEstimate(flops=8 * 10**9, bytes_accessed=10**7, transcendentals=10**6),
    )(
        in_map,
        tile_w.reshape(3, 3 * CH, CH),
        head_w1.reshape(3, 3 * CH, CH),
        head_w2.reshape(3, 3 * CH, CH),
        box_row.T,
        box_col.T,
        box_target.T,
        head_cot[:, 0].transpose(1, 2, 0, 3),
    )
    grad_map, first, second = pl.pallas_call(
        finish,
        out_shape=(
            jax.ShapeDtypeStruct((16, 32, CH), BF),
            jax.ShapeDtypeStruct((9, CH, CH), F32),
            jax.ShapeDtypeStruct((9, CH, CH), F32),
        ),
        in_specs=[in_any] * 2,
        out_specs=(in_any,) * 3,
        scratch_shapes=[
            vm((2, 2, 9, CH, 128), BF),
            vm((2, 9, CH, CH), F32),
            pltpu.SemaphoreType.DMA((3,)),
            pltpu.SemaphoreType.DMA((6,)),
            pltpu.SemaphoreType.DMA,
        ],
        compiler_params=pltpu.CompilerParams(vmem_limit_bytes=58 * 1024 * 1024),
    )(grad_map, sums)
    return grad_map, first.reshape(3, 3, CH, CH), second.reshape(3, 3, CH, CH)


def solution(mesh):
    in_specs = (
        P("row", "col", None),
        P(),
        P(),
        P(),
        P("row", "col"),
        P("row", "col"),
        P("row", "col"),
        P("row", "col", None, None, None),
    )
    out_specs = (P("row", "col", None), P(), P())
    return jax.shard_map(step, mesh=mesh, in_specs=in_specs, out_specs=out_specs, check_vma=False)
```

```python
import math

import jax
import jax.numpy as jnp
from jax import lax
from jax.experimental import pallas as pl
from jax.experimental.pallas import tpu as pltpu
from jax.sharding import PartitionSpec as P

MESH = pl.DeviceIdType.MESH
BF = jnp.bfloat16
F32 = jnp.float32
NZ = 8
NX = 4
NY = 4
NROW = 32
PX = 512
HALF = 256
POS = 256
CH = 256
K_HALO = 0
K_TAB = 16
K_AG = 23
K_RS = 37
K_AR = 51
AR_N = 33
N_SEM = K_AR + 4 * AR_N
PARTS = ((1, 0, 5, False), (1, 5, 4, True), (0, 0, 5, True), (0, 5, 4, False))


def silu_slope(values):
    sigma = jax.nn.sigmoid(values)
    return sigma * (1.0 + values * (1.0 - sigma))


def mm(a, b):
    return jnp.dot(a, b, preferred_element_type=F32)


def kernel(
    in_ref, tw_any, w1_any, w2_any, brow_ref, bcol_ref, btgt_ref, cot_any,
    gmap_ref, gsum_ref,
    tw_ref, w1_ref, w2_ref, cot_ref, xf, xp, x3m, slope_map, scol, hrow, hcol, hl, hr,
    tab, gcol, grow, feats, acc, xc3, xh3, d23, d13, slope1, cotf, cots, xt,
    twt, w1t, w2t, bg, rs_s, rs_r, dm,
    own, snd, rc, s1, r1, t2, s2, r2, t3, s3, r3, zb,
    ssem, rsem, lsem,
):
    row = lax.axis_index("row")
    me = lax.axis_index("col")
    px = row // 8
    py = lax.rem(row // 2, NY)
    core = lax.rem(row, 2)

    def at_x(d):
        return (lax.rem(px + d, NX) * 8 + py * 2 + core, me)

    def at_y(d):
        return (px * 8 + lax.rem(py + d, NY) * 2 + core, me)

    def at_z(d):
        return (row, lax.rem(me + d + NZ, NZ))

    sibling = (row + 1 - 2 * core, me)

    def near(dr, dc):
        return (lax.rem(row + dr + NROW, NROW), lax.rem(me + dc + NZ, NZ))

    live = {}

    def send(src, dst, k, dev):
        copy = pltpu.make_async_remote_copy(
            src_ref=src, dst_ref=dst, send_sem=ssem.at[k], recv_sem=rsem.at[k],
            device_id=dev, device_id_type=MESH,
        )
        copy.start()
        live[k] = copy

    def got(k):
        live[k].wait_recv()

    halo_dirs = [(1, 0), (-1, 0), (1, 1), (0, 1), (-1, 1), (1, -1), (0, -1), (-1, -1)]

    barrier = pltpu.get_barrier_semaphore()
    partners = [near(*d) for d in halo_dirs]
    partners += [at_z(d) for d in range(2, 7)]
    partners += [at_x(d) for d in range(1, 4)] + [at_y(d) for d in range(1, 4)] + [sibling]
    for dev in partners:
        pl.semaphore_signal(barrier, inc=1, device_id=dev, device_id_type=MESH)

    loads = []
    for n, (src, dst) in enumerate(
        ((tw_any, tw_ref), (w2_any, w2_ref), (w1_any, w1_ref), (cot_any, cot_ref))
    ):
        loads.append(pltpu.make_async_copy(src, dst, lsem.at[n]))
        loads[n].start()

    xf[...] = in_ref[...].astype(F32)
    scol[0, 0] = xf[:, 31, :].astype(BF)
    scol[0, 1] = xf[:, 0, :].astype(BF)
    tab[0] = jnp.full((8, 128), -128, jnp.int32)
    tab[0, 0:1, 0:16] = btgt_ref[...] * 128 + brow_ref[...] * 32 + bcol_ref[...]
    xp[pl.ds(32, PX), :] = in_ref[...].reshape(PX, CH)

    pl.semaphore_wait(barrier, len(partners))

    def halo_send(t, img):
        base = K_HALO + 8 * t
        for i, d in enumerate(halo_dirs):
            if i < 2:
                send(img.at[15 if i == 0 else 0], hrow.at[t, i], base + i, near(*d))
            else:
                send(scol.at[t, 0 if i < 5 else 1], hcol.at[t, i - 2], base + i, near(*d))

    def halo_recv(t):
        base = K_HALO + 8 * t
        for i in range(8):
            got(base + i)
        above, below = row > 0, row < NROW - 1
        left, right = me > 0, me < NZ - 1

        def part(ok, v):
            return jnp.where(ok, v, jnp.zeros_like(v))

        xp[pl.ds(0, 32), :] = part(above, hrow[t, 0])
        xp[pl.ds(544, 32), :] = part(below, hrow[t, 1])
        for side, ok, dst in ((0, left, hl), (3, right, hr)):
            dst[0:1, :] = part(ok & above, hcol[t, side].astype(F32)[15:16, :])
            dst[1:17, :] = part(ok, hcol[t, side + 1].astype(F32))
            dst[17:18, :] = part(ok & below, hcol[t, side + 2].astype(F32)[0:1, :])

        lanes = lax.broadcasted_iota(jnp.int32, (32, CH), 0)

        def one(r, carry):
            at = pl.multiple_of(r * 32, 32)
            mid = xp[pl.ds(at, 32), :]
            c = mid.astype(F32)
            lf = jnp.where(lanes == 0, hl[pl.ds(r, 1), :], pltpu.roll(c, 1, 0))
            rt = jnp.where(lanes == 31, hr[pl.ds(r, 1), :], pltpu.roll(c, 31, 0))
            x3m[pl.ds(at, 32), 0:CH] = lf.astype(BF)
            x3m[pl.ds(at, 32), CH:2 * CH] = mid
            x3m[pl.ds(at, 32), 2 * CH:3 * CH] = rt.astype(BF)
            return carry

        return one

    def conv_map(w, j):
        total = mm(x3m[pl.ds(j * HALF, HALF), :], w[0])
        total += mm(x3m[pl.ds(j * HALF + 32, HALF), :], w[1])
        total += mm(x3m[pl.ds(j * HALF + 64, HALF), :], w[2])
        return total

    def turn(src, dst, taps):
        for a in taps:
            for b in range(3):
                dst[a, b * CH:(b + 1) * CH, :] = src[2 - a, (2 - b) * CH:(3 - b) * CH, :].T

    halo_send(0, in_ref)
    for d in range(1, NZ):
        send(tab.at[0], tab.at[d], K_TAB + d - 1, at_z(d))
    for buf in (xc3, xh3, d23, d13):
        for h in range(5):
            at = max(h * POS, 0)
            buf[at:at + 32, :] = jnp.zeros((32, 3 * CH), BF)
    acc[...] = jnp.zeros_like(acc)
    loads[1].wait()
    turn(w2_ref, w2t, (0, 1, 2))
    loads[0].wait()
    widen = halo_recv(0)

    def ag_key(right, s, j):
        return K_AG + (0 if right else 7) + (s * 2 + j if s < 3 else 6)

    def ag_send(right, s, j):
        src = feats.at[s if right else (NZ - s) % NZ, pl.ds(j * HALF, HALF), :]
        dst = feats.at[s + 1 if right else NZ - 1 - s, pl.ds(j * HALF, HALF), :]
        send(src, dst, ag_key(right, s, j), at_z(1 if right else -1))

    for j in range(2):
        lax.fori_loop(10 * j, 10 + 8 * j, widen, 0)
        pre = conv_map(tw_ref, j)
        feats[0, pl.ds(j * HALF, HALF), :] = (pre * jax.nn.sigmoid(pre)).astype(BF)
        ag_send(True, 0, j)
        ag_send(False, 0, j)
        slope_map[pl.ds(j * HALF, HALF), :] = silu_slope(pre)

    for d in range(1, NZ):
        got(K_TAB + d - 1)
    for h in range(4):
        base = jnp.zeros((1, 1), jnp.int32)
        for s in range(NZ):
            tile = lax.rem(me - s + NZ, NZ)
            word = tab[s, 0:1, :]
            hit = (word >> 7) == me * 4 + h
            value = (word & 127) + tile * PX
            base += jnp.sum(jnp.where(hit, value, 0), axis=1, keepdims=True)
        p = lax.broadcasted_iota(jnp.int32, (POS, 128), 0)
        i, j = p >> 4, p & 15
        ok = (i >= 1) & (i <= 14) & (j < 14)
        gcol[h] = jnp.where(ok, base + (i - 1) * 32 + j, -1)
        p = lax.broadcasted_iota(jnp.int32, (1, POS), 1)
        i, j = p >> 4, p & 15
        ok = (i >= 1) & (i <= 14) & (j < 14)
        grow[0:1, h * POS:(h + 1) * POS] = jnp.where(ok, base + (i - 1) * 32 + j, -1)

    def take(s, j):
        tile = lax.rem(me - s + NZ, NZ)
        first = tile * PX + j * HALF

        def one(h, carry):
            q = lax.broadcasted_iota(jnp.int32, (POS, 128), 1) + first
            g = gcol[h]
            hot = jnp.concatenate(
                [jnp.where(g == q, 1.0, 0.0), jnp.where(g == q + 128, 1.0, 0.0)], axis=1
            ).astype(BF)
            acc[h] += mm(hot, feats[s, pl.ds(j * HALF, HALF), :])
            return carry

        lax.fori_loop(0, 4, one, 0)

    take(0, 0)
    take(0, 1)

    loads[2].wait()
    loads[3].wait()

    def spread(i, carry):
        cotf[...] = cot_ref[i].astype(F32)
        for h in range(4):
            cots[h, i, 0:14, :] = cotf[:, h, :]
            cots[h, i, 14:16, :] = jnp.zeros((2, CH), F32)
        return carry

    lax.fori_loop(0, 14, spread, 0)
    for s in range(1, 4):
        for j in range(2):
            got(ag_key(True, s - 1, j))
            if s < 3 or j == 0:
                ag_send(True, s, j)
            got(ag_key(False, s - 1, j))
            if s < 3 or j == 1:
                ag_send(False, s, j)
            take(s, j)
            take(NZ - s, j)
            if s < 3:
                n = 2 * (s - 1) + j
                if n < 3:
                    turn(w1_ref, w1t, (n,))
                turn(tw_ref, twt, (n,) if n < 3 else ())
    got(ag_key(True, 3, 0))
    take(4, 0)
    got(ag_key(False, 3, 1))
    take(4, 1)

    inside = (lax.broadcasted_iota(jnp.int32, (224, CH), 0) & 15) < 14

    def put(buf, h, value):
        at = h * POS + 32
        mid = value.astype(BF)
        full = mid.astype(F32)
        buf[pl.ds(at, 224), 0:CH] = pltpu.roll(full, 1, 0).astype(BF)
        buf[pl.ds(at, 224), CH:2 * CH] = mid
        buf[pl.ds(at, 224), 2 * CH:3 * CH] = pltpu.roll(full, 223, 0).astype(BF)

    def conv_box(buf, w, h):
        at = h * POS + 16
        total = mm(buf[pl.ds(at, 224), :], w[0])
        total += mm(buf[pl.ds(at + 16, 224), :], w[1])
        total += mm(buf[pl.ds(at + 32, 224), :], w[2])
        return total

    def cut(v):
        return jnp.where(inside, v, 0.0)

    for h in range(4):
        put(xc3, h, acc[h, 16:240, :])
    for h in range(4):
        pre = conv_box(xc3, w1_ref, h)
        put(xh3, h, cut(pre * jax.nn.sigmoid(pre)))
        slope1[h] = silu_slope(pre)
    for h in range(4):
        pre = conv_box(xh3, w2_ref, h)
        put(d23, h, cut(cots[h].reshape(224, CH) * silu_slope(pre)))

    def term(d, j):
        tile = lax.rem(me + d + NZ, NZ)
        q = lax.broadcasted_iota(jnp.int32, (HALF, 4 * POS), 0) + (tile * PX + j * HALF)
        hot = jnp.where(q == grow[0:1, :], 1.0, 0.0).astype(BF)
        return mm(hot, bg[...])

    def rs_item(right, k):
        if k == 0:
            d, j = 4, 0
        else:
            d = 3 - (k - 1) // 2
            j = 1 if k % 2 == 1 else 0
        return d, (j if right else 1 - j)

    def rs_key(right, k):
        return K_RS + (0 if right else 7) + k

    def rs_step(k):
        for right in (True, False):
            d, j = rs_item(right, k)
            side = 0 if right else 1
            value = term(d if right else -d, j)
            if k >= 2:
                got(rs_key(right, k - 2))
                value += rs_r[side, k - 2].astype(F32)
            rs_s[side, k] = value.astype(BF)
            send(rs_s.at[side, k], rs_r.at[side, k], rs_key(right, k), at_z(1 if right else -1))

    def wgrad(g, buf, dbuf):
        for h in range(4):
            xt[:, h * POS:(h + 1) * POS] = buf[16 + h * POS:16 + (h + 1) * POS, CH:2 * CH].T

        for a in range(3):
            at = 32 - a * 16
            for b in range(3):
                value = mm(xt[...], dbuf[pl.ds(at, 4 * POS), (2 - b) * CH:(3 - b) * CH])
                low, high = value[:, 0:128], value[:, 128:256]
                own[g, a * 3 + b] = jnp.where(core == 0, low, high)
                snd[g, a * 3 + b] = jnp.where(core == 0, high, low).astype(BF)
            if a > 0:
                n = 2 * (1 - g) + a - 1
                span = pl.ds(PARTS[n][1], PARTS[n][2])
                send(snd.at[g, span], rc.at[g, span], K_AR + n * AR_N, sibling)

    def axes(n):
        if PARTS[n][3]:
            return at_x, px, NX, at_y, py, NY
        return at_y, py, NY, at_x, px, NX

    def ar1(n):
        g, t0, nt, _ = PARTS[n]
        k = K_AR + n * AR_N
        at1, p1, n1 = axes(n)[:3]
        got(k)

        def one(t, carry):
            v = own[g, t] + rc[g, t].astype(F32)
            own[g, t] = v
            s1[g, t] = v.astype(BF)
            return carry

        lax.fori_loop(t0, t0 + nt, one, 0)
        for d in range(1, 4):
            q = lax.rem(p1 + d, n1)
            src = s1.at[g, pl.ds(t0, nt), pl.ds(q * 64, 64), :]
            send(src, r1.at[n, d - 1, pl.ds(0, nt)], k + d, at1(d))

    def ar2(n):
        g, t0, nt, _ = PARTS[n]
        k = K_AR + n * AR_N
        at1, p1, n1, at2, p2, n2 = axes(n)
        for d in range(1, 4):
            got(k + d)

        def one(t, carry):
            v = own[g, t0 + t, pl.ds(p1 * 64, 64), :]
            for d in range(3):
                v += r1[n, d, t].astype(F32)
            t2[n, t] = v
            s2[n, t] = v.astype(BF)
            return carry

        lax.fori_loop(0, nt, one, 0)
        for d in range(1, 4):
            q = lax.rem(p2 + d, n2)
            src = s2.at[n, pl.ds(0, nt), pl.ds(q * 16, 16), :]
            send(src, r2.at[n, d - 1, pl.ds(0, nt)], k + 3 + d, at2(d))

    def owner(n, t):
        return t + (0 if PARTS[n][1] == 0 else 4)

    def z_copy(src, dst, ks, kr, to):
        return pltpu.make_async_remote_copy(
            src_ref=src, dst_ref=dst, send_sem=ssem.at[ks], recv_sem=rsem.at[kr],
            device_id=(row, to), device_id_type=MESH,
        )

    def ar3(n):
        nt = PARTS[n][2]
        k = K_AR + n * AR_N
        p2 = axes(n)[4]
        for d in range(1, 4):
            got(k + 3 + d)
        v = t2[n, 0:nt, pl.ds(p2 * 16, 16), :]
        for d in range(3):
            v += r2[n, d, 0:nt].astype(F32)
        t3[n, 0:nt] = v
        s3[n, 0:nt] = v.astype(BF)
        for t in range(nt):
            to = owner(n, t)

            @pl.when(me != to)
            def _():
                z_copy(s3.at[n, t], r3.at[n, me], k + 7 + t, k + 7 + me, to).start()

    def ar4(n):
        nt = PARTS[n][2]
        k = K_AR + n * AR_N
        first = owner(n, 0)

        @pl.when((me >= first) & (me < first + nt))
        def _():
            for p in range(NZ):
                @pl.when(me != p)
                def _():
                    z_copy(s3.at[n, 0], r3.at[n, p], k + 7, k + 7 + p, p).wait_recv()
            v = t3[n, me - first]
            for p in range(NZ):
                v += jnp.where(me != p, r3[n, p].astype(F32), 0.0)
            zb[n, me - first] = v.astype(BF)
            part = zb.at[n, me - first]
            for p in range(NZ):
                @pl.when(me != p)
                def _():
                    z_copy(part, part, k + 15 + p, k + 15 + me - first, p).start()

    def ar5(n):
        g, t0, nt, _ = PARTS[n]
        k = K_AR + n * AR_N
        at1, p1, n1, at2, p2, n2 = axes(n)
        first = owner(n, 0)
        for t in range(nt):
            @pl.when(me != owner(n, t))
            def _():
                z_copy(zb.at[n, t], zb.at[n, t], k + 15, k + 15 + t, owner(n, t)).wait_recv()
        at = pl.multiple_of(p1 * 64 + p2 * 16, 16)
        gsum_ref[g, core, t0:t0 + nt, pl.ds(at, 16), :] = zb[n, 0:nt]
        part = gsum_ref.at[g, core, pl.ds(t0, nt), pl.ds(at, 16), :]
        for d in range(1, 4):
            send(part, part, k + 22 + d, at2(d))

    def z_sent(n):
        nt = PARTS[n][2]
        k = K_AR + n * AR_N
        first = owner(n, 0)
        for t in range(nt):
            @pl.when(me != owner(n, t))
            def _():
                z_copy(s3.at[n, t], r3.at[n, me], k + 7 + t, k + 7, owner(n, t)).wait_send()

        @pl.when((me >= first) & (me < first + nt))
        def _():
            for p in range(NZ):
                @pl.when(me != p)
                def _():
                    z_copy(zb.at[n, 0], zb.at[n, 0], k + 15 + p, k + 15, p).wait_send()

    def ar6(n):
        g, t0, nt, _ = PARTS[n]
        k = K_AR + n * AR_N
        at1, p1, n1 = axes(n)[:3]
        for d in range(1, 4):
            got(k + 22 + d)
        part = gsum_ref.at[g, core, pl.ds(t0, nt), pl.ds(p1 * 64, 64), :]
        for d in range(1, 4):
            send(part, part, k + 25 + d, at1(d))
        send(part, part, k + 29, sibling)

    def ar7(n):
        g, t0, nt, _ = PARTS[n]
        k = K_AR + n * AR_N
        at1, p1, n1 = axes(n)[:3]
        for d in (1, 3, 2):
            got(k + 25 + d)
            q = lax.rem(p1 - d + n1, n1)
            part = gsum_ref.at[g, core, pl.ds(t0, nt), pl.ds(q * 64, 64), :]
            send(part, part, k + 29 + d, sibling)

    def both(stage, g):
        stage(2 * (1 - g))
        stage(2 * (1 - g) + 1)

    wgrad(1, xh3, d23)
    for h in range(4):
        put(d13, h, cut(conv_box(d23, w2t, h) * slope1[h]))
    wgrad(0, xc3, d13)
    both(ar1, 1)
    for h in range(4):
        bg[h * POS:h * POS + 16, :] = jnp.zeros((16, CH), BF)
        bg[h * POS + 240:(h + 1) * POS, :] = jnp.zeros((16, CH), BF)
        bg[h * POS + 16:h * POS + 240, :] = conv_box(d13, w1t, h).astype(BF)
    rs_step(0)
    both(ar1, 0)
    rs_step(1)
    both(ar2, 1)
    rs_step(2)
    both(ar2, 0)
    both(ar3, 1)
    both(ar3, 0)
    rs_step(3)
    both(ar4, 1)
    rs_step(4)
    both(ar4, 0)
    both(ar5, 1)
    rs_step(5)
    both(ar5, 0)
    both(ar6, 1)
    rs_step(6)
    both(ar6, 0)
    both(ar7, 1)

    for j in range(2):
        total = term(0, j)
        for right in (True, False):
            k = 6 if rs_item(right, 6)[1] == j else 5
            got(rs_key(right, k))
            total += rs_r[0 if right else 1, k].astype(F32)
        grad = (total * slope_map[pl.ds(j * HALF, HALF), :]).astype(BF)
        xp[pl.ds(32 + j * HALF, HALF), :] = grad
        dm[8 * j:8 * j + 8] = grad.reshape(8, 32, CH)
        xf[8 * j:8 * j + 8] = grad.astype(F32).reshape(8, 32, CH)
    scol[1, 0] = xf[:, 31, :].astype(BF)
    scol[1, 1] = xf[:, 0, :].astype(BF)
    halo_send(1, dm)
    both(ar7, 0)
    lax.fori_loop(0, 18, halo_recv(1), 0)
    for j in range(2):
        gmap_ref[8 * j:8 * j + 8] = conv_map(twt, j).astype(BF).reshape(8, 32, CH)
    for n in range(4):
        for d in range(4):
            got(K_AR + n * AR_N + 29 + d)
        z_sent(n)
    for k in sorted(live):
        live[k].wait_send()


def finish(map_ref, sums_ref, out_ref, first_ref, second_ref, held, made, kept, isem, osem, msem):
    factor = 1.0 / math.sqrt(32 * 8 * 4 * 14 * 14)
    bring = pltpu.make_async_copy(map_ref, kept, msem.at[0])
    bring.start()
    loads, stores = [], []
    for t in range(3):
        span = pl.ds(3 * t, 3)
        loads.append(pltpu.make_async_copy(sums_ref.at[:, :, span], held.at[:, :, span], isem.at[t]))
        loads[t].start()
    for t in range(3):
        loads[t].wait()
        for g, ref in enumerate((first_ref, second_ref)):
            for half in range(2):
                low = half * 128
                made[g, 3 * t:3 * t + 3, :, low:low + 128] = (
                    held[g, half, 3 * t:3 * t + 3].astype(F32) * factor
                )
            span = pl.ds(3 * t, 3)
            store = pltpu.make_async_copy(made.at[g, span], ref.at[span], osem.at[2 * t + g])
            store.start()
            stores.append(store)
    bring.wait()
    store = pltpu.make_async_copy(kept, out_ref, msem.at[1])
    store.start()
    stores.append(store)
    for store in stores:
        store.wait()


def step(in_map, tile_w, head_w1, head_w2, box_row, box_col, box_target, head_cot):
    vm = pltpu.VMEM
    scratch = [
        vm((3, 3 * CH, CH), BF),
        vm((3, 3 * CH, CH), BF),
        vm((3, 3 * CH, CH), BF),
        vm((14, 14, 4, CH), BF),
        vm((16, 32, CH), F32),
        vm((576, CH), BF),
        vm((576, 3 * CH), BF),
        vm((PX, CH), F32),
        vm((2, 2, 16, CH), BF),
        vm((2, 2, 32, CH), BF),
        vm((2, 6, 16, CH), BF),
        vm((24, CH), F32),
        vm((24, CH), F32),
        vm((NZ, 8, 128), jnp.int32),
        vm((4, POS, 128), jnp.int32),
        vm((1, 4 * POS), jnp.int32),
        vm((NZ, PX, CH), BF),
        vm((4, POS, CH), F32),
        vm((1056, 3 * CH), BF),
        vm((1056, 3 * CH), BF),
        vm((1056, 3 * CH), BF),
        vm((1056, 3 * CH), BF),
        vm((4, 224, CH), F32),
        vm((14, 4, CH), F32),
        vm((4, 14, 16, CH), F32),
        vm((CH, 4 * POS), BF),
        vm((3, 3 * CH, CH), BF),
        vm((3, 3 * CH, CH), BF),
        vm((3, 3 * CH, CH), BF),
        vm((4 * POS, CH), BF),
        vm((2, 7, HALF, CH), BF),
        vm((2, 7, HALF, CH), BF),
        vm((16, 32, CH), BF),
        vm((2, 9, 256, 128), F32),
        vm((2, 9, 256, 128), BF),
        vm((2, 9, 256, 128), BF),
        vm((2, 9, 256, 128), BF),
        vm((4, 3, 5, 64, 128), BF),
        vm((4, 5, 64, 128), F32),
        vm((4, 5, 64, 128), BF),
        vm((4, 3, 5, 16, 128), BF),
        vm((4, 5, 16, 128), F32),
        vm((4, 5, 16, 128), BF),
        vm((4, NZ, 16, 128), BF),
        vm((4, 5, 16, 128), BF),
        pltpu.SemaphoreType.DMA((N_SEM,)),
        pltpu.SemaphoreType.DMA((N_SEM,)),
        pltpu.SemaphoreType.DMA((4,)),
    ]
    in_vmem = pl.BlockSpec(memory_space=pltpu.VMEM)
    in_any = pl.BlockSpec(memory_space=pl.ANY)
    grad_map, sums = pl.pallas_call(
        kernel,
        out_shape=(
            jax.ShapeDtypeStruct((16, 32, CH), BF),
            jax.ShapeDtypeStruct((2, 2, 9, 256, 128), BF),
        ),
        in_specs=[in_vmem] + [in_any] * 3 + [in_vmem] * 3 + [in_any],
        out_specs=(in_vmem, in_vmem),
        scratch_shapes=scratch,
        compiler_params=pltpu.CompilerParams(
            collective_id=0, has_side_effects=True, vmem_limit_bytes=58 * 1024 * 1024
        ),
        cost_estimate=pl.CostEstimate(flops=8 * 10**9, bytes_accessed=10**7, transcendentals=10**6),
    )(
        in_map,
        tile_w.reshape(3, 3 * CH, CH),
        head_w1.reshape(3, 3 * CH, CH),
        head_w2.reshape(3, 3 * CH, CH),
        box_row.T,
        box_col.T,
        box_target.T,
        head_cot[:, 0].transpose(1, 2, 0, 3),
    )
    grad_map, first, second = pl.pallas_call(
        finish,
        out_shape=(
            jax.ShapeDtypeStruct((16, 32, CH), BF),
            jax.ShapeDtypeStruct((9, CH, CH), F32),
            jax.ShapeDtypeStruct((9, CH, CH), F32),
        ),
        in_specs=[in_any] * 2,
        out_specs=(in_any,) * 3,
        scratch_shapes=[
            vm((2, 2, 9, CH, 128), BF),
            vm((2, 9, CH, CH), F32),
            vm((16, 32, CH), BF),
            pltpu.SemaphoreType.DMA((3,)),
            pltpu.SemaphoreType.DMA((6,)),
            pltpu.SemaphoreType.DMA((2,)),
        ],
        compiler_params=pltpu.CompilerParams(vmem_limit_bytes=58 * 1024 * 1024),
    )(grad_map, sums)
    return grad_map, first.reshape(3, 3, CH, CH), second.reshape(3, 3, CH, CH)


def solution(mesh):
    in_specs = (
        P("row", "col", None),
        P(),
        P(),
        P(),
        P("row", "col"),
        P("row", "col"),
        P("row", "col"),
        P("row", "col", None, None, None),
    )
    out_specs = (P("row", "col", None), P(), P())
    return jax.shard_map(step, mesh=mesh, in_specs=in_specs, out_specs=out_specs, check_vma=False)
```

```python
import math

import jax
import jax.numpy as jnp
from jax import lax
from jax.experimental import pallas as pl
from jax.experimental.pallas import tpu as pltpu
from jax.sharding import PartitionSpec as P

MESH = pl.DeviceIdType.MESH
BF = jnp.bfloat16
F32 = jnp.float32
NZ = 8
NX = 4
NY = 4
NROW = 32
PX = 512
HALF = 256
POS = 256
CH = 256
K_HALO = 0
K_TAB = 16
K_AG = 23
K_RS = 37
K_AR = 51
AR_N = 33
N_SEM = K_AR + 4 * AR_N
PARTS = ((1, 0, 5, False), (1, 5, 4, True), (0, 0, 5, True), (0, 5, 4, False))


def silu_slope(values):
    sigma = jax.nn.sigmoid(values)
    return sigma * (1.0 + values * (1.0 - sigma))


def mm(a, b):
    return jnp.dot(a, b, preferred_element_type=F32)


def kernel(
    in_ref, tw_any, w1_any, w2_any, brow_ref, bcol_ref, btgt_ref, cot_any,
    gmap_ref, gsum_ref,
    tw_ref, w1_ref, w2_ref, cot_ref, xf, xp, x3m, slope_map, scol, hrow, hcol, hl, hr,
    tab, gcol, grow, feats, acc, xc3, xh3, d23, d13, slope1, cotf, cots, xt,
    twt, w1t, w2t, bg, rs_s, rs_r, dm,
    own, snd, rc, s1, r1, t2, s2, r2, t3, s3, r3, zb,
    ssem, rsem, lsem,
):
    row = lax.axis_index("row")
    me = lax.axis_index("col")
    px = row // 8
    py = lax.rem(row // 2, NY)
    core = lax.rem(row, 2)

    def at_x(d):
        return (lax.rem(px + d, NX) * 8 + py * 2 + core, me)

    def at_y(d):
        return (px * 8 + lax.rem(py + d, NY) * 2 + core, me)

    def at_z(d):
        return (row, lax.rem(me + d + NZ, NZ))

    sibling = (row + 1 - 2 * core, me)

    def near(dr, dc):
        return (lax.rem(row + dr + NROW, NROW), lax.rem(me + dc + NZ, NZ))

    live = {}

    def send(src, dst, k, dev):
        copy = pltpu.make_async_remote_copy(
            src_ref=src, dst_ref=dst, send_sem=ssem.at[k], recv_sem=rsem.at[k],
            device_id=dev, device_id_type=MESH,
        )
        copy.start()
        live[k] = copy

    def got(k):
        live[k].wait_recv()

    halo_dirs = [(1, 0), (-1, 0), (1, 1), (0, 1), (-1, 1), (1, -1), (0, -1), (-1, -1)]

    barrier = pltpu.get_barrier_semaphore()
    partners = [near(*d) for d in halo_dirs]
    partners += [at_z(d) for d in range(2, 7)]
    partners += [at_x(d) for d in range(1, 4)] + [at_y(d) for d in range(1, 4)] + [sibling]
    for dev in partners:
        pl.semaphore_signal(barrier, inc=1, device_id=dev, device_id_type=MESH)

    loads = []
    for n, (src, dst) in enumerate(
        ((tw_any, tw_ref), (w2_any, w2_ref), (w1_any, w1_ref), (cot_any, cot_ref))
    ):
        loads.append(pltpu.make_async_copy(src, dst, lsem.at[n]))
        loads[n].start()

    xf[...] = in_ref[...].astype(F32)
    scol[0, 0] = xf[:, 31, :].astype(BF)
    scol[0, 1] = xf[:, 0, :].astype(BF)
    tab[0] = jnp.full((8, 128), -128, jnp.int32)
    tab[0, 0:1, 0:16] = btgt_ref[...] * 128 + brow_ref[...] * 32 + bcol_ref[...]
    xp[pl.ds(32, PX), :] = in_ref[...].reshape(PX, CH)

    pl.semaphore_wait(barrier, len(partners))

    def halo_send(t, img):
        base = K_HALO + 8 * t
        for i, d in enumerate(halo_dirs):
            if i < 2:
                send(img.at[15 if i == 0 else 0], hrow.at[t, i], base + i, near(*d))
            else:
                send(scol.at[t, 0 if i < 5 else 1], hcol.at[t, i - 2], base + i, near(*d))

    def halo_recv(t):
        base = K_HALO + 8 * t
        for i in range(8):
            got(base + i)
        above, below = row > 0, row < NROW - 1
        left, right = me > 0, me < NZ - 1

        def part(ok, v):
            return jnp.where(ok, v, jnp.zeros_like(v))

        xp[pl.ds(0, 32), :] = part(above, hrow[t, 0])
        xp[pl.ds(544, 32), :] = part(below, hrow[t, 1])
        for side, ok, dst in ((0, left, hl), (3, right, hr)):
            dst[0:1, :] = part(ok & above, hcol[t, side].astype(F32)[15:16, :])
            dst[1:17, :] = part(ok, hcol[t, side + 1].astype(F32))
            dst[17:18, :] = part(ok & below, hcol[t, side + 2].astype(F32)[0:1, :])

        lanes = lax.broadcasted_iota(jnp.int32, (32, CH), 0)

        def one(r, carry):
            at = pl.multiple_of(r * 32, 32)
            mid = xp[pl.ds(at, 32), :]
            c = mid.astype(F32)
            lf = jnp.where(lanes == 0, hl[pl.ds(r, 1), :], pltpu.roll(c, 1, 0))
            rt = jnp.where(lanes == 31, hr[pl.ds(r, 1), :], pltpu.roll(c, 31, 0))
            x3m[pl.ds(at, 32), 0:CH] = lf.astype(BF)
            x3m[pl.ds(at, 32), CH:2 * CH] = mid
            x3m[pl.ds(at, 32), 2 * CH:3 * CH] = rt.astype(BF)
            return carry

        return one

    def conv_map(w, j):
        total = mm(x3m[pl.ds(j * HALF, HALF), :], w[0])
        total += mm(x3m[pl.ds(j * HALF + 32, HALF), :], w[1])
        total += mm(x3m[pl.ds(j * HALF + 64, HALF), :], w[2])
        return total

    def turn(src, dst, taps):
        for a in taps:
            for b in range(3):
                dst[a, b * CH:(b + 1) * CH, :] = src[2 - a, (2 - b) * CH:(3 - b) * CH, :].T

    halo_send(0, in_ref)
    for d in range(1, NZ):
        send(tab.at[0], tab.at[d], K_TAB + d - 1, at_z(d))
    for buf in (xc3, xh3, d23, d13):
        for h in range(5):
            at = max(h * POS, 0)
            buf[at:at + 32, :] = jnp.zeros((32, 3 * CH), BF)
    acc[...] = jnp.zeros_like(acc)
    loads[1].wait()
    turn(w2_ref, w2t, (0, 1, 2))
    loads[0].wait()
    widen = halo_recv(0)

    def ag_key(right, s, j):
        return K_AG + (0 if right else 7) + (s * 2 + j if s < 3 else 6)

    def ag_send(right, s, j):
        src = feats.at[s if right else (NZ - s) % NZ, pl.ds(j * HALF, HALF), :]
        dst = feats.at[s + 1 if right else NZ - 1 - s, pl.ds(j * HALF, HALF), :]
        send(src, dst, ag_key(right, s, j), at_z(1 if right else -1))

    for j in range(2):
        lax.fori_loop(10 * j, 10 + 8 * j, widen, 0)
        pre = conv_map(tw_ref, j)
        feats[0, pl.ds(j * HALF, HALF), :] = (pre * jax.nn.sigmoid(pre)).astype(BF)
        ag_send(True, 0, j)
        ag_send(False, 0, j)
        slope_map[pl.ds(j * HALF, HALF), :] = silu_slope(pre)

    for d in range(1, NZ):
        got(K_TAB + d - 1)
    for h in range(4):
        base = jnp.zeros((1, 1), jnp.int32)
        for s in range(NZ):
            tile = lax.rem(me - s + NZ, NZ)
            word = tab[s, 0:1, :]
            hit = (word >> 7) == me * 4 + h
            value = (word & 127) + tile * PX
            base += jnp.sum(jnp.where(hit, value, 0), axis=1, keepdims=True)
        p = lax.broadcasted_iota(jnp.int32, (POS, 128), 0)
        i, j = p >> 4, p & 15
        ok = (i >= 1) & (i <= 14) & (j < 14)
        gcol[h] = jnp.where(ok, base + (i - 1) * 32 + j, -1)
        p = lax.broadcasted_iota(jnp.int32, (1, POS), 1)
        i, j = p >> 4, p & 15
        ok = (i >= 1) & (i <= 14) & (j < 14)
        grow[0:1, h * POS:(h + 1) * POS] = jnp.where(ok, base + (i - 1) * 32 + j, -1)

    def take(s, j):
        tile = lax.rem(me - s + NZ, NZ)
        first = tile * PX + j * HALF

        def one(h, carry):
            q = lax.broadcasted_iota(jnp.int32, (POS, 128), 1) + first
            g = gcol[h]
            hot = jnp.concatenate(
                [jnp.where(g == q, 1.0, 0.0), jnp.where(g == q + 128, 1.0, 0.0)], axis=1
            ).astype(BF)
            acc[h] += mm(hot, feats[s, pl.ds(j * HALF, HALF), :])
            return carry

        lax.fori_loop(0, 4, one, 0)

    take(0, 0)
    take(0, 1)

    loads[2].wait()
    loads[3].wait()

    def spread(i, carry):
        cotf[...] = cot_ref[i].astype(F32)
        for h in range(4):
            cots[h, i, 0:14, :] = cotf[:, h, :]
            cots[h, i, 14:16, :] = jnp.zeros((2, CH), F32)
        return carry

    lax.fori_loop(0, 14, spread, 0)
    for s in range(1, 4):
        for j in range(2):
            got(ag_key(True, s - 1, j))
            if s < 3 or j == 0:
                ag_send(True, s, j)
            got(ag_key(False, s - 1, j))
            if s < 3 or j == 1:
                ag_send(False, s, j)
            take(s, j)
            take(NZ - s, j)
            if s < 3:
                n = 2 * (s - 1) + j
                if n < 3:
                    turn(w1_ref, w1t, (n,))
                turn(tw_ref, twt, (n,) if n < 3 else ())
    got(ag_key(True, 3, 0))
    take(4, 0)
    got(ag_key(False, 3, 1))
    take(4, 1)

    inside = (lax.broadcasted_iota(jnp.int32, (224, CH), 0) & 15) < 14

    def put(buf, h, value):
        at = h * POS + 32
        mid = value.astype(BF)
        full = mid.astype(F32)
        buf[pl.ds(at, 224), 0:CH] = pltpu.roll(full, 1, 0).astype(BF)
        buf[pl.ds(at, 224), CH:2 * CH] = mid
        buf[pl.ds(at, 224), 2 * CH:3 * CH] = pltpu.roll(full, 223, 0).astype(BF)

    def conv_box(buf, w, h):
        at = h * POS + 16
        total = mm(buf[pl.ds(at, 224), :], w[0])
        total += mm(buf[pl.ds(at + 16, 224), :], w[1])
        total += mm(buf[pl.ds(at + 32, 224), :], w[2])
        return total

    def cut(v):
        return jnp.where(inside, v, 0.0)

    for h in range(4):
        put(xc3, h, acc[h, 16:240, :])
    for h in range(4):
        pre = conv_box(xc3, w1_ref, h)
        put(xh3, h, cut(pre * jax.nn.sigmoid(pre)))
        slope1[h] = silu_slope(pre)
    for h in range(4):
        pre = conv_box(xh3, w2_ref, h)
        put(d23, h, cut(cots[h].reshape(224, CH) * silu_slope(pre)))

    def term(d, j):
        tile = lax.rem(me + d + NZ, NZ)
        q = lax.broadcasted_iota(jnp.int32, (HALF, 4 * POS), 0) + (tile * PX + j * HALF)
        hot = jnp.where(q == grow[0:1, :], 1.0, 0.0).astype(BF)
        return mm(hot, bg[...])

    def rs_item(right, k):
        if k == 0:
            d, j = 4, 0
        else:
            d = 3 - (k - 1) // 2
            j = 1 if k % 2 == 1 else 0
        return d, (j if right else 1 - j)

    def rs_key(right, k):
        return K_RS + (0 if right else 7) + k

    def rs_step(k):
        work = []
        for right in (True, False):
            d, j = rs_item(right, k)
            work.append((right, term(d if right else -d, j)))
        for right, value in work:
            side = 0 if right else 1
            if k >= 2:
                got(rs_key(right, k - 2))
                value += rs_r[side, k - 2].astype(F32)
            rs_s[side, k] = value.astype(BF)
            send(rs_s.at[side, k], rs_r.at[side, k], rs_key(right, k), at_z(1 if right else -1))

    def wgrad(g, buf, dbuf):
        for h in range(4):
            xt[:, h * POS:(h + 1) * POS] = buf[16 + h * POS:16 + (h + 1) * POS, CH:2 * CH].T

        for a in range(3):
            at = 32 - a * 16
            for b in range(3):
                value = mm(xt[...], dbuf[pl.ds(at, 4 * POS), (2 - b) * CH:(3 - b) * CH])
                low, high = value[:, 0:128], value[:, 128:256]
                own[g, a * 3 + b] = jnp.where(core == 0, low, high)
                snd[g, a * 3 + b] = jnp.where(core == 0, high, low).astype(BF)
            if a > 0:
                n = 2 * (1 - g) + a - 1
                span = pl.ds(PARTS[n][1], PARTS[n][2])
                send(snd.at[g, span], rc.at[g, span], K_AR + n * AR_N, sibling)

    def axes(n):
        if PARTS[n][3]:
            return at_x, px, NX, at_y, py, NY
        return at_y, py, NY, at_x, px, NX

    def ar1(n):
        g, t0, nt, _ = PARTS[n]
        k = K_AR + n * AR_N
        at1, p1, n1 = axes(n)[:3]
        got(k)

        def one(t, carry):
            v = own[g, t] + rc[g, t].astype(F32)
            own[g, t] = v
            s1[g, t] = v.astype(BF)
            return carry

        lax.fori_loop(t0, t0 + nt, one, 0)
        for d in range(1, 4):
            q = lax.rem(p1 + d, n1)
            src = s1.at[g, pl.ds(t0, nt), pl.ds(q * 64, 64), :]
            send(src, r1.at[n, d - 1, pl.ds(0, nt)], k + d, at1(d))

    def ar2(n):
        g, t0, nt, _ = PARTS[n]
        k = K_AR + n * AR_N
        at1, p1, n1, at2, p2, n2 = axes(n)
        for d in range(1, 4):
            got(k + d)

        def one(t, carry):
            v = own[g, t0 + t, pl.ds(p1 * 64, 64), :]
            for d in range(3):
                v += r1[n, d, t].astype(F32)
            t2[n, t] = v
            s2[n, t] = v.astype(BF)
            return carry

        lax.fori_loop(0, nt, one, 0)
        for d in range(1, 4):
            q = lax.rem(p2 + d, n2)
            src = s2.at[n, pl.ds(0, nt), pl.ds(q * 16, 16), :]
            send(src, r2.at[n, d - 1, pl.ds(0, nt)], k + 3 + d, at2(d))

    def owner(n, t):
        return t + (0 if PARTS[n][1] == 0 else 4)

    def z_copy(src, dst, ks, kr, to):
        return pltpu.make_async_remote_copy(
            src_ref=src, dst_ref=dst, send_sem=ssem.at[ks], recv_sem=rsem.at[kr],
            device_id=(row, to), device_id_type=MESH,
        )

    def ar3(n):
        nt = PARTS[n][2]
        k = K_AR + n * AR_N
        p2 = axes(n)[4]
        for d in range(1, 4):
            got(k + 3 + d)
        v = t2[n, 0:nt, pl.ds(p2 * 16, 16), :]
        for d in range(3):
            v += r2[n, d, 0:nt].astype(F32)
        t3[n, 0:nt] = v
        s3[n, 0:nt] = v.astype(BF)
        for t in range(nt):
            to = owner(n, t)

            @pl.when(me != to)
            def _():
                z_copy(s3.at[n, t], r3.at[n, me], k + 7 + t, k + 7 + me, to).start()

    def ar4(n):
        nt = PARTS[n][2]
        k = K_AR + n * AR_N
        first = owner(n, 0)

        @pl.when((me >= first) & (me < first + nt))
        def _():
            for p in range(NZ):
                @pl.when(me != p)
                def _():
                    z_copy(s3.at[n, 0], r3.at[n, p], k + 7, k + 7 + p, p).wait_recv()
            v = t3[n, me - first]
            for p in range(NZ):
                v += jnp.where(me != p, r3[n, p].astype(F32), 0.0)
            zb[n, me - first] = v.astype(BF)
            part = zb.at[n, me - first]
            for p in range(NZ):
                @pl.when(me != p)
                def _():
                    z_copy(part, part, k + 15 + p, k + 15 + me - first, p).start()

    def ar5(n):
        g, t0, nt, _ = PARTS[n]
        k = K_AR + n * AR_N
        at1, p1, n1, at2, p2, n2 = axes(n)
        first = owner(n, 0)
        for t in range(nt):
            @pl.when(me != owner(n, t))
            def _():
                z_copy(zb.at[n, t], zb.at[n, t], k + 15, k + 15 + t, owner(n, t)).wait_recv()
        at = pl.multiple_of(p1 * 64 + p2 * 16, 16)
        gsum_ref[g, core, t0:t0 + nt, pl.ds(at, 16), :] = zb[n, 0:nt]
        part = gsum_ref.at[g, core, pl.ds(t0, nt), pl.ds(at, 16), :]
        for d in range(1, 4):
            send(part, part, k + 22 + d, at2(d))

    def z_sent(n):
        nt = PARTS[n][2]
        k = K_AR + n * AR_N
        first = owner(n, 0)
        for t in range(nt):
            @pl.when(me != owner(n, t))
            def _():
                z_copy(s3.at[n, t], r3.at[n, me], k + 7 + t, k + 7, owner(n, t)).wait_send()

        @pl.when((me >= first) & (me < first + nt))
        def _():
            for p in range(NZ):
                @pl.when(me != p)
                def _():
                    z_copy(zb.at[n, 0], zb.at[n, 0], k + 15 + p, k + 15, p).wait_send()

    def ar6(n):
        g, t0, nt, _ = PARTS[n]
        k = K_AR + n * AR_N
        at1, p1, n1 = axes(n)[:3]
        for d in range(1, 4):
            got(k + 22 + d)
        part = gsum_ref.at[g, core, pl.ds(t0, nt), pl.ds(p1 * 64, 64), :]
        for d in range(1, 4):
            send(part, part, k + 25 + d, at1(d))
        send(part, part, k + 29, sibling)

    def ar7(n):
        g, t0, nt, _ = PARTS[n]
        k = K_AR + n * AR_N
        at1, p1, n1 = axes(n)[:3]
        for d in (1, 3, 2):
            got(k + 25 + d)
            q = lax.rem(p1 - d + n1, n1)
            part = gsum_ref.at[g, core, pl.ds(t0, nt), pl.ds(q * 64, 64), :]
            send(part, part, k + 29 + d, sibling)

    def both(stage, g):
        stage(2 * (1 - g))
        stage(2 * (1 - g) + 1)

    wgrad(1, xh3, d23)
    for h in range(4):
        put(d13, h, cut(conv_box(d23, w2t, h) * slope1[h]))
    wgrad(0, xc3, d13)
    both(ar1, 1)
    for h in range(4):
        bg[h * POS:h * POS + 16, :] = jnp.zeros((16, CH), BF)
        bg[h * POS + 240:(h + 1) * POS, :] = jnp.zeros((16, CH), BF)
        bg[h * POS + 16:h * POS + 240, :] = conv_box(d13, w1t, h).astype(BF)
    rs_step(0)
    both(ar1, 0)
    rs_step(1)
    both(ar2, 1)
    rs_step(2)
    both(ar2, 0)
    both(ar3, 1)
    both(ar3, 0)
    rs_step(3)
    both(ar4, 1)
    rs_step(4)
    both(ar4, 0)
    both(ar5, 1)
    rs_step(5)
    both(ar5, 0)
    both(ar6, 1)
    rs_step(6)
    both(ar6, 0)
    both(ar7, 1)

    for j in range(2):
        total = term(0, j)
        for right in (True, False):
            k = 6 if rs_item(right, 6)[1] == j else 5
            got(rs_key(right, k))
            total += rs_r[0 if right else 1, k].astype(F32)
        grad = (total * slope_map[pl.ds(j * HALF, HALF), :]).astype(BF)
        xp[pl.ds(32 + j * HALF, HALF), :] = grad
        dm[8 * j:8 * j + 8] = grad.reshape(8, 32, CH)
        xf[8 * j:8 * j + 8] = grad.astype(F32).reshape(8, 32, CH)
    scol[1, 0] = xf[:, 31, :].astype(BF)
    scol[1, 1] = xf[:, 0, :].astype(BF)
    halo_send(1, dm)
    both(ar7, 0)
    lax.fori_loop(0, 18, halo_recv(1), 0)
    for j in range(2):
        gmap_ref[8 * j:8 * j + 8] = conv_map(twt, j).astype(BF).reshape(8, 32, CH)
    for n in range(4):
        for d in range(4):
            got(K_AR + n * AR_N + 29 + d)
        z_sent(n)
    for k in sorted(live):
        live[k].wait_send()


def finish(map_ref, sums_ref, out_ref, first_ref, second_ref, held, made, kept, isem, osem, msem):
    factor = 1.0 / math.sqrt(32 * 8 * 4 * 14 * 14)
    bring = pltpu.make_async_copy(map_ref, kept, msem.at[0])
    bring.start()
    loads, stores = [], []
    for t in range(3):
        span = pl.ds(3 * t, 3)
        loads.append(pltpu.make_async_copy(sums_ref.at[:, :, span], held.at[:, :, span], isem.at[t]))
        loads[t].start()
    for t in range(3):
        loads[t].wait()
        for g, ref in enumerate((first_ref, second_ref)):
            for half in range(2):
                low = half * 128
                made[g, 3 * t:3 * t + 3, :, low:low + 128] = (
                    held[g, half, 3 * t:3 * t + 3].astype(F32) * factor
                )
            span = pl.ds(3 * t, 3)
            store = pltpu.make_async_copy(made.at[g, span], ref.at[span], osem.at[2 * t + g])
            store.start()
            stores.append(store)
    bring.wait()
    store = pltpu.make_async_copy(kept, out_ref, msem.at[1])
    store.start()
    stores.append(store)
    for store in stores:
        store.wait()


def step(in_map, tile_w, head_w1, head_w2, box_row, box_col, box_target, head_cot):
    vm = pltpu.VMEM
    scratch = [
        vm((3, 3 * CH, CH), BF),
        vm((3, 3 * CH, CH), BF),
        vm((3, 3 * CH, CH), BF),
        vm((14, 14, 4, CH), BF),
        vm((16, 32, CH), F32),
        vm((576, CH), BF),
        vm((576, 3 * CH), BF),
        vm((PX, CH), F32),
        vm((2, 2, 16, CH), BF),
        vm((2, 2, 32, CH), BF),
        vm((2, 6, 16, CH), BF),
        vm((24, CH), F32),
        vm((24, CH), F32),
        vm((NZ, 8, 128), jnp.int32),
        vm((4, POS, 128), jnp.int32),
        vm((1, 4 * POS), jnp.int32),
        vm((NZ, PX, CH), BF),
        vm((4, POS, CH), F32),
        vm((1056, 3 * CH), BF),
        vm((1056, 3 * CH), BF),
        vm((1056, 3 * CH), BF),
        vm((1056, 3 * CH), BF),
        vm((4, 224, CH), F32),
        vm((14, 4, CH), F32),
        vm((4, 14, 16, CH), F32),
        vm((CH, 4 * POS), BF),
        vm((3, 3 * CH, CH), BF),
        vm((3, 3 * CH, CH), BF),
        vm((3, 3 * CH, CH), BF),
        vm((4 * POS, CH), BF),
        vm((2, 7, HALF, CH), BF),
        vm((2, 7, HALF, CH), BF),
        vm((16, 32, CH), BF),
        vm((2, 9, 256, 128), F32),
        vm((2, 9, 256, 128), BF),
        vm((2, 9, 256, 128), BF),
        vm((2, 9, 256, 128), BF),
        vm((4, 3, 5, 64, 128), BF),
        vm((4, 5, 64, 128), F32),
        vm((4, 5, 64, 128), BF),
        vm((4, 3, 5, 16, 128), BF),
        vm((4, 5, 16, 128), F32),
        vm((4, 5, 16, 128), BF),
        vm((4, NZ, 16, 128), BF),
        vm((4, 5, 16, 128), BF),
        pltpu.SemaphoreType.DMA((N_SEM,)),
        pltpu.SemaphoreType.DMA((N_SEM,)),
        pltpu.SemaphoreType.DMA((4,)),
    ]
    in_vmem = pl.BlockSpec(memory_space=pltpu.VMEM)
    in_any = pl.BlockSpec(memory_space=pl.ANY)
    grad_map, sums = pl.pallas_call(
        kernel,
        out_shape=(
            jax.ShapeDtypeStruct((16, 32, CH), BF),
            jax.ShapeDtypeStruct((2, 2, 9, 256, 128), BF),
        ),
        in_specs=[in_vmem] + [in_any] * 3 + [in_vmem] * 3 + [in_any],
        out_specs=(in_vmem, in_vmem),
        scratch_shapes=scratch,
        compiler_params=pltpu.CompilerParams(
            collective_id=0, has_side_effects=True, vmem_limit_bytes=58 * 1024 * 1024
        ),
        cost_estimate=pl.CostEstimate(flops=8 * 10**9, bytes_accessed=10**7, transcendentals=10**6),
    )(
        in_map,
        tile_w.reshape(3, 3 * CH, CH),
        head_w1.reshape(3, 3 * CH, CH),
        head_w2.reshape(3, 3 * CH, CH),
        box_row.T,
        box_col.T,
        box_target.T,
        head_cot[:, 0].transpose(1, 2, 0, 3),
    )
    grad_map, first, second = pl.pallas_call(
        finish,
        out_shape=(
            jax.ShapeDtypeStruct((16, 32, CH), BF),
            jax.ShapeDtypeStruct((9, CH, CH), F32),
            jax.ShapeDtypeStruct((9, CH, CH), F32),
        ),
        in_specs=[in_any] * 2,
        out_specs=(in_any,) * 3,
        scratch_shapes=[
            vm((2, 2, 9, CH, 128), BF),
            vm((2, 9, CH, CH), F32),
            vm((16, 32, CH), BF),
            pltpu.SemaphoreType.DMA((3,)),
            pltpu.SemaphoreType.DMA((6,)),
            pltpu.SemaphoreType.DMA((2,)),
        ],
        compiler_params=pltpu.CompilerParams(vmem_limit_bytes=58 * 1024 * 1024),
    )(grad_map, sums)
    return grad_map, first.reshape(3, 3, CH, CH), second.reshape(3, 3, CH, CH)


def solution(mesh):
    in_specs = (
        P("row", "col", None),
        P(),
        P(),
        P(),
        P("row", "col"),
        P("row", "col"),
        P("row", "col"),
        P("row", "col", None, None, None),
    )
    out_specs = (P("row", "col", None), P(), P())
    return jax.shard_map(step, mesh=mesh, in_specs=in_specs, out_specs=out_specs, check_vma=False)
```
